256 devices in a mesh: dp: 8 (over z), table: 32 (over y, x, core).
Axes of the slice: x: 4, y: 4, z: 8, core: 2. Of those that a mesh axis runs over, the one named last changes fastest.
Arguments:
- owners: int32 [512, 1024, 1], P(('dp', 'table')), may hold values from 0 to 31; in each aligned block of 1024 rows (0 to 1023, 1024 to 2047, ..., all dimensions but the last counted through in order) at most 48 rows name the same one
- local_rows: int32 [512, 1024], P(('dp', 'table')), may hold values from 0 to 4095
- lengths: int32 [512], P(('dp', 'table')), may hold values from 256 to 1024, as said below
- destinations: int32 [32, 16], P('table', 'dp'), may hold values from 0 to 15, each once within a row
- table: bfloat16 [131072, 512], P('table'), may hold values from -6 to 6
- gain_in: float32 [512], replicated, may hold values from 0.5 to 1.5
- w_in: bfloat16 [512, 2048], replicated, may hold values from -0.25 to 0.25
- b_in: float32 [2048], replicated, may hold values from -3 to 3
- gain_out: float32 [512], replicated, may hold values from 0.5 to 1.5
- w_out: bfloat16 [512, 512], replicated, may hold values from -0.25 to 0.25
- b_out: float32 [512], replicated, may hold values from -3 to 3
Outputs:
- layer_out: bfloat16 [512, 1024, 512], P(('dp', 'table'))
The draws below stay inside these ranges and needn't reach their ends.
Inputs may be any that keep to these rules, and one draw needn't show every extreme that they name: `owners`: in the 1024 events of one history no table shard is named more than 48 times; this many is reached in some histories. `lengths`: some history of every draw has exactly 1024 events. `destinations`: each row is a permutation of the 16 slots along dp.
All inputs are finite; a program needn't handle non-finite values.
Results may differ from the reference program's by a relative error of at most 0.0045.
Values may be sent and summed in bfloat16 or wider, within the bound.
A program may use at most 128 MiB of HBM per device.

```python
import math
import jax
import jax.numpy as jnp
import numpy as np
from jax import lax

D = 512
HEADS = 8
LMAX = 1024
TILE = 256
SEQ_DEV = 2
ROWS_DEV = 4096
SEQS = 512
TABLE_ROWS = 131072
CAP_SEQ = 48
N_DP = 8
N_TABLE = 32


def draw_lengths(key, part):
    key = jax.random.fold_in(key, 11)
    drawn = jax.random.randint(key, (SEQS,), TILE, LMAX + 1, dtype=jnp.int32)
    return drawn.at[0].set(LMAX)


def with_ends(values, key, least, top_value):
    index_at = [jax.random.randint(jax.random.fold_in(key, axis), (), 0, length) for axis, length in enumerate(values.shape)]
    longest = values.shape.index(max(values.shape))
    beside = index_at[:longest] + [(index_at[longest] + 1) % values.shape[longest]] + index_at[longest + 1:]
    return values.at[tuple(index_at)].set(least).at[tuple(beside)].set(top_value)


def steps_of(key, dims, split, least, high):
    def one(axis_at, shards_of):
        heights = jax.random.uniform(jax.random.fold_in(jax.random.fold_in(key, 6), axis_at), (shards_of,), jnp.float32, least / len(split), high / len(split))
        return jnp.repeat(jnp.exp(heights), dims[axis_at] // shards_of).reshape((-1,) + (1,) * (len(dims) - axis_at - 1))

    level = one(*split[0])
    for cut in split[1:]:
        level = level * one(*cut)
    return level


def deal_out(stream_key, own, number, rows, count, top, reach, lean):
    order = jax.random.permutation(stream_key, count)
    packed, ordinary = load_shares(count, rows * top, reach, lean, True), load_shares(count, rows * top, reach, lean, False)
    places = jnp.arange(count)

    def named(sizes, turn):
        used = int((sizes > 0).sum())
        fixed = max(1, used // 4)
        passed = fixed + (places - fixed + turn * (used - fixed)) % max(1, count - fixed)
        return jnp.zeros((count,), jnp.int32).at[order[jnp.where(places < fixed, places, passed)]].set(jnp.asarray(sizes, jnp.int32))

    sizes = jnp.where(number % 4 == 0, named(packed, number // 4), named(ordinary, number - number // 4 - 1))
    mixed = jax.random.permutation(jax.random.fold_in(own, 3), count)
    giver, receiver = mixed[0:count // 2 * 2:2], mixed[1:count // 2 * 2:2]
    room = jnp.minimum(sizes[giver] - 1, reach - sizes[receiver]) // 2
    room = jnp.where((giver == order[0]) | (receiver == order[0]) | (sizes[receiver] == 0), 0, jnp.maximum(room, 0))
    passed = jax.random.randint(jax.random.fold_in(own, 4), (count // 2,), 0, 1 << 20) % (room + 1)
    sizes = sizes.at[giver].add(-passed).at[receiver].add(passed)
    items = jnp.searchsorted(jnp.cumsum(sizes), jnp.arange(rows * top), side="right").astype(jnp.int32)
    listing = items.reshape(top, rows).T
    listing = listing[jax.random.permutation(jax.random.fold_in(own, 1), rows)]
    turn = jax.random.randint(jax.random.fold_in(own, 2), (rows, 1), 0, top)
    return jnp.take_along_axis(listing, (jnp.arange(top)[None, :] + turn) % top, axis=1)


def load_shares(count, total, limit, lean, full):
    weights = [(1 << 20) // math.isqrt(grade ** lean) + 1 for grade in range(1, count + 1)]
    largest = limit if full else min(limit, max(-(-total // count), total * weights[0] // sum(weights)))
    least = 1 if total - largest >= count - 1 else 0
    holding, surplus = [largest] + [least] * (count - 1), total - largest - least * (count - 1)
    while surplus > 0:
        candidates = [i for i in range(1, count) if holding[i] < largest] or [i for i in range(1, count) if holding[i] < limit]
        mass, left = sum([weights[i] for i in candidates]), surplus
        for i in candidates:
            more = min(limit - holding[i], max(1, left * weights[i] // mass), surplus)
            holding[i] = holding[i] + more
            surplus = surplus - more
    return np.array(holding)


def gaussian(stream_key, dims, scale, reach, split=(), kind=jnp.bfloat16):
    entries = scale * jax.random.normal(stream_key, dims, jnp.float32)
    if split:
        entries = entries * steps_of(stream_key, dims, split, -0.22, 0.18)
    return jnp.clip(entries, -reach, reach).astype(kind)


def setup_inputs(seed: int = 0) -> dict:
    seeds = jax.random.split(jax.random.key(seed), 12)
    owners_keys = jax.random.split(jax.random.fold_in(seeds[0], 1), SEQS * LMAX // LMAX)
    owners_turns = jax.random.permutation(jax.random.fold_in(seeds[0], 3), SEQS * LMAX // LMAX)
    owners = jax.vmap(lambda own, number: deal_out(jax.random.fold_in(seeds[0], 2), own, number, LMAX, N_TABLE, 1, CAP_SEQ, 2))(owners_keys, owners_turns).reshape((SEQS, LMAX, 1))
    local_rows = with_ends(jax.random.randint(seeds[1], (SEQS, LMAX), 0, ROWS_DEV), jax.random.fold_in(seeds[1], 1), 0, ROWS_DEV - 1).astype(jnp.int32)
    lengths = draw_lengths(jax.random.fold_in(seeds[11], 71), 0)
    destinations = jax.vmap(lambda own: jax.random.permutation(own, N_DP * SEQ_DEV))(jax.random.split(seeds[3], N_TABLE)).reshape((N_TABLE, N_DP * SEQ_DEV)).astype(jnp.int32)
    table = gaussian(seeds[4], (TABLE_ROWS, D), 1.0, 6.0, ((0, 32),))
    gain_in = jnp.clip(1.0 + 0.1 * jax.random.normal(seeds[5], (D,), jnp.float32), 0.5, 1.5)
    w_in = gaussian(seeds[6], (D, 4 * D), D ** -0.5, 0.25)
    b_in = gaussian(seeds[7], (4 * D,), 0.5, 3.0, (), jnp.float32)
    gain_out = jnp.clip(1.0 + 0.1 * jax.random.normal(seeds[8], (D,), jnp.float32), 0.5, 1.5)
    w_out = gaussian(seeds[9], (D, D), D ** -0.5, 0.25)
    b_out = gaussian(seeds[10], (D,), 0.5, 3.0, (), jnp.float32)
    return {"owners": owners, "local_rows": local_rows, "lengths": lengths, "destinations": destinations, "table": table, "gain_in": gain_in, "w_in": w_in, "b_in": b_in, "gain_out": gain_out, "w_out": w_out, "b_out": b_out}


score_scale = 0.125
norm_eps = 1e-05

def layer_norm(values, gain_vec):
    centre = lax.optimization_barrier(jnp.mean(values, axis=-1, keepdims=True))
    spread = values - centre
    variance = lax.optimization_barrier(jnp.mean(spread * spread, axis=-1, keepdims=True))
    return spread * lax.rsqrt(variance + norm_eps) * gain_vec

def hstu_layer(history, length, gain_in, w_in, b_in, gain_out, w_out, b_out):
    events = history.shape[0]
    model_width = history.shape[1]
    head_size = model_width // HEADS
    hist_float = history.astype(jnp.float32)
    normed = layer_norm(hist_float, gain_in).astype(jnp.bfloat16)
    active = jax.nn.silu(jnp.dot(normed, w_in, preferred_element_type=jnp.float32) + b_in)
    gate_part = active[:, :model_width]
    value_part = active[:, model_width:2 * model_width].astype(jnp.bfloat16).reshape(events, HEADS, head_size)
    query_part = active[:, 2 * model_width:3 * model_width].astype(jnp.bfloat16).reshape(events, HEADS, head_size)
    key_part = active[:, 3 * model_width:].astype(jnp.bfloat16).reshape(events, HEADS, head_size)
    block_rows = min(512, events)
    position = jnp.arange(events)
    pieces = []
    for block_id in range(events // block_rows):
        first = block_id * block_rows
        query_block = query_part[first:first + block_rows].astype(jnp.float32)
        scores = jnp.einsum('qhd,khd->hqk', query_block, key_part.astype(jnp.float32))
        query_pos = position[first:first + block_rows]
        allowed = (position[None, :] <= query_pos[:, None]) & (position[None, :] < length)
        weights = jnp.where(allowed[None], jax.nn.silu(scores * score_scale), 0.0).astype(jnp.bfloat16)
        pieces.append(jnp.einsum('hqk,khd->qhd', weights.astype(jnp.float32), value_part.astype(jnp.float32)))
    attended = jnp.concatenate(pieces, 0).reshape(events, model_width)
    gated_rows = (layer_norm(attended, gain_out) * gate_part).astype(jnp.bfloat16)
    update = jnp.dot(gated_rows, w_out, preferred_element_type=jnp.float32) + b_out
    return jnp.where(position[:, None] < length, hist_float + update, 0.0).astype(jnp.bfloat16)

def reference(owners, local_rows, lengths, destinations, table, gain_in, w_in, b_in, gain_out, w_out, b_out):
    anchor = jnp.arange(SEQS, dtype=jnp.int32)
    column = anchor // SEQ_DEV % N_TABLE
    within = anchor // (SEQ_DEV * N_TABLE) * SEQ_DEV + anchor % SEQ_DEV
    target = destinations[column, within].astype(jnp.int32)
    landing = (target // SEQ_DEV * N_TABLE + column) * SEQ_DEV + target % SEQ_DEV
    source = jnp.zeros((SEQS,), jnp.int32).at[landing].set(anchor)

    def one_history(sequence):
        length = lengths[sequence]
        row_ids = owners[sequence, :, 0] * ROWS_DEV + local_rows[sequence]
        found_rows = jnp.take(table, row_ids, axis=0)
        present = jnp.arange(LMAX) < length
        history = jnp.where(present[:, None], found_rows, 0).astype(jnp.bfloat16)
        return hstu_layer(history, length, gain_in, w_in, b_in, gain_out, w_out, b_out)
    return lax.map(one_history, source)
```

```python
import functools
import jax
import jax.numpy as jnp
from jax import lax
from jax.experimental import pallas as pl
from jax.experimental.pallas import tpu as pltpu
from jax.sharding import PartitionSpec as P

HEADS = 8
EPS = 1e-05
BLK = 256
BF = jnp.bfloat16
F32 = jnp.float32


def silu_half(u):
    return u + u * jnp.tanh(u)


def norm_rows(values, gain):
    centre = jnp.mean(values, axis=-1, keepdims=True)
    spread = values - centre
    variance = jnp.mean(spread * spread, axis=-1, keepdims=True)
    return spread * lax.rsqrt(variance + EPS) * gain


def layer_kernel(slot_ref, rows_ref, gain_in_ref, w_in_ref, b_in_ref, gain_out_ref, w_out_ref, b_out_ref,
                 out_ref, hist, gate, q, k, v0, v1, att):
    events, width = hist.shape
    slots = rows_ref.shape[0]
    lanes = lax.broadcasted_iota(jnp.int32, (128, 128), 1)
    subs = lax.broadcasted_iota(jnp.int32, (128, 128), 0)
    eye = lanes == subs
    half = lax.broadcasted_iota(jnp.int32, (BLK, 128), 1) < 64

    def project(c, carry):
        cols = []
        for i in range(BLK // 128):
            line = slot_ref[pl.ds(c * (BLK // 128) + i, 1), :]
            spread = jnp.where(eye, jnp.broadcast_to(line, (128, 128)), 0)
            cols.append(jnp.sum(spread, axis=1, keepdims=True))
        col = jnp.concatenate(cols, axis=0)
        here = (col >= 0).astype(F32)
        pick = (col == lax.broadcasted_iota(jnp.int32, (BLK, slots), 1)).astype(F32).astype(BF)
        rows = jnp.dot(pick, rows_ref[...], preferred_element_type=F32)
        at = pl.ds(pl.multiple_of(c * BLK, BLK), BLK)
        hist[at, :] = rows.astype(BF)
        normed = norm_rows(rows, gain_in_ref[...]).astype(BF)
        for part in range(4):
            cs = slice(part * width, (part + 1) * width)
            pre = jnp.dot(normed, w_in_ref[:, cs], preferred_element_type=F32) + b_in_ref[:, cs]
            act = silu_half(0.5 * pre)
            if part == 0:
                gate[at, :] = act
            elif part == 1:
                act = act * here
                for p in range(4):
                    piece = act[:, p * 128:(p + 1) * 128]
                    v0[p, at, :] = jnp.where(half, piece, 0.0).astype(BF)
                    v1[p, at, :] = jnp.where(half, 0.0, piece).astype(BF)
            else:
                target = q if part == 2 else k
                act = act.astype(BF)
                for p in range(4):
                    target[p, at, :] = act[:, p * 128:(p + 1) * 128]
        return carry

    lax.fori_loop(0, events // BLK, project, 0)

    tri = lax.broadcasted_iota(jnp.int32, (BLK, BLK), 0) >= lax.broadcasted_iota(jnp.int32, (BLK, BLK), 1)

    def attend(p, carry):
        for i in range(events // BLK):
            at = slice(i * BLK, (i + 1) * BLK)
            qb = q[p, at, :] * jnp.bfloat16(0.0625)
            total = None
            for h, v in ((0, v0), (1, v1)):
                qh = jnp.where(half == (h == 0), qb.astype(F32), 0.0).astype(BF)
                for j in range(i + 1):
                    ks = slice(j * BLK, (j + 1) * BLK)
                    s = lax.dot_general(qh, k[p, ks, :], (((1,), (1,)), ((), ())), preferred_element_type=F32)
                    w = silu_half(s)
                    if j == i:
                        w = jnp.where(tri, w, 0.0)
                    o = jnp.dot(w.astype(BF), v[p, ks, :], preferred_element_type=F32)
                    total = o if total is None else total + o
            att[p, at, :] = total
        return carry

    lax.fori_loop(0, 4, attend, 0)

    def finish(c, carry):
        cols = []
        for i in range(BLK // 128):
            line = slot_ref[pl.ds(c * (BLK // 128) + i, 1), :]
            spread = jnp.where(eye, jnp.broadcast_to(line, (128, 128)), 0)
            cols.append(jnp.sum(spread, axis=1, keepdims=True))
        here = jnp.concatenate(cols, axis=0) >= 0
        at = pl.ds(pl.multiple_of(c * BLK, BLK), BLK)
        full = jnp.concatenate([att[p, at, :] for p in range(4)], axis=1)
        gated = (norm_rows(full, gain_out_ref[...]) * gate[at, :]).astype(BF)
        update = jnp.dot(gated, w_out_ref[...], preferred_element_type=F32) + b_out_ref[...]
        out_ref[0, at, :] = jnp.where(here, hist[at, :].astype(F32) + update, 0.0).astype(BF)
        return carry

    lax.fori_loop(0, events // BLK, finish, 0)


def layer_call(s, slot, rows, gain_in, w_in, b_in, gain_out, w_out, b_out, before):
    events = slot.shape[0] * 128
    width = rows.shape[1]
    vm = pl.BlockSpec(memory_space=pltpu.VMEM)
    ins = [slot, rows, gain_in[None], w_in, b_in[None], gain_out[None], w_out, b_out[None]]
    specs = [vm] * len(ins)
    kernel = layer_kernel
    aliases = {}
    if before is not None:
        ins.append(before)
        specs.append(pl.BlockSpec(memory_space=pl.ANY))
        aliases = {len(ins) - 1: 0}

        def kernel(*refs):
            layer_kernel(*refs[:8], *refs[9:])
    return pl.pallas_call(
        kernel,
        grid=(1,),
        in_specs=specs,
        out_specs=pl.BlockSpec((1, events, width), lambda i: (s, 0, 0)),
        out_shape=jax.ShapeDtypeStruct((2, events, width), BF),
        scratch_shapes=[
            pltpu.VMEM((events, width), BF),
            pltpu.VMEM((events, width), F32),
            pltpu.VMEM((4, events, 128), BF),
            pltpu.VMEM((4, events, 128), BF),
            pltpu.VMEM((4, events, 128), BF),
            pltpu.VMEM((4, events, 128), BF),
            pltpu.VMEM((4, events, 128), F32),
        ],
        input_output_aliases=aliases,
        compiler_params=pltpu.CompilerParams(vmem_limit_bytes=40 << 20),
        cost_estimate=pl.CostEstimate(flops=8 * 10**9, bytes_accessed=8 << 20, transcendentals=8 << 20),
        name="layer",
    )(*ins)
MESH = pl.DeviceIdType.MESH
SLOTS = 48
INT = jnp.int32


def route_kernel(seqs, n_dp, n_table, owners_ref, rows_ref, lengths_ref, dest_ref, asked_ref, slot_ref,
                 mine, every, req, send_z, recv_z, send_t, recv_t):
    me_dp, me_t = lax.axis_index("dp"), lax.axis_index("table")
    events = owners_ref.shape[1]
    lines = events // 128
    barrier = pltpu.get_barrier_semaphore()
    for i in range(1, n_dp):
        pl.semaphore_signal(barrier, inc=1, device_id={"dp": lax.rem(me_dp + i, n_dp)}, device_id_type=MESH)

    @pl.loop(1, n_table)
    def _(i):
        pl.semaphore_signal(barrier, inc=1, device_id={"table": lax.rem(me_t + i, n_table)}, device_id_type=MESH)

    lane = lax.broadcasted_iota(INT, (1, 128), 1)
    for s in range(seqs):
        for r in range(lines):
            cs = slice(r * 128, (r + 1) * 128)
            packed = owners_ref[s:s + 1, cs] * 4096 + rows_ref[s:s + 1, cs]
            mine[s * lines + r:s * lines + r + 1, :] = jnp.where(lane + r * 128 < lengths_ref[s], packed, -1)
    for j in range(8):
        mine[seqs * lines + j:seqs * lines + j + 1, :] = jnp.zeros((1, 128), INT) + dest_ref[0, min(j, seqs - 1)]
    every[me_dp] = mine[...]
    pl.semaphore_wait(barrier, n_dp - 1 + n_table - 1)

    copies = []
    for i in range(1, n_dp):
        copy = pltpu.make_async_remote_copy(
            src_ref=mine, dst_ref=every.at[me_dp], send_sem=send_z.at[i], recv_sem=recv_z.at[me_dp],
            device_id={"dp": lax.rem(me_dp + i, n_dp)}, device_id_type=MESH)
        copy.start()
        copies.append(copy)
    for i in range(1, n_dp):
        pltpu.make_async_remote_copy(
            src_ref=mine, dst_ref=every.at[lax.rem(me_dp + i, n_dp)], send_sem=send_z.at[i],
            recv_sem=recv_z.at[lax.rem(me_dp + i, n_dp)],
            device_id={"dp": lax.rem(me_dp + i, n_dp)}, device_id_type=MESH).wait_recv()

    shard = lax.broadcasted_iota(INT, (n_table, 128), 0)
    place = lax.broadcasted_iota(INT, (128, 128), 0)
    upper = (place <= lax.broadcasted_iota(INT, (128, 128), 1)).astype(F32).astype(BF)
    request = jnp.zeros((2 * n_table, 128), F32)
    for s in range(seqs):
        refs = jnp.zeros((lines, 128), INT)
        for d in range(n_dp):
            for j in range(seqs):
                went = every[d, seqs * lines + j:seqs * lines + j + 1, :]
                refs += jnp.where(went == me_dp * seqs + s, every[d, j * lines:(j + 1) * lines, :], 0)
        owner, row = refs >> 12, refs & 4095
        named = [(jnp.broadcast_to(owner[r:r + 1, :], (n_table, 128)) == shard) for r in range(lines)]
        before = jnp.zeros((n_table, 1), F32)
        for r in range(lines):
            hot = named[r].astype(F32)
            upto = jnp.dot(hot.astype(BF), upper, preferred_element_type=F32) + before
            before += jnp.sum(hot, axis=1, keepdims=True)
            rank = jnp.sum(jnp.where(named[r], upto - 1.0, 0.0), axis=0, keepdims=True)
            slot = jnp.sum(jnp.where(named[r], upto + (shard * SLOTS).astype(F32), 0.0), axis=0, keepdims=True)
            slot_ref[s, r:r + 1, :] = slot.astype(INT) - 1
            high = jnp.broadcast_to(row[r:r + 1, :] >> 6, (n_table, 128)).astype(F32)
            low = jnp.broadcast_to(row[r:r + 1, :] & 63, (n_table, 128)).astype(F32)
            left = jnp.concatenate([jnp.where(named[r], high, 0.0), jnp.where(named[r], low, 0.0)], axis=0)
            right = jnp.broadcast_to(rank.astype(INT) + s * SLOTS, (128, 128)) == place
            request += lax.dot_general(left.astype(BF), right.astype(F32).astype(BF), (((1,), (1,)), ((), ())),
                                       preferred_element_type=F32)
    wanted = (request[:n_table] * 64.0 + request[n_table:]).astype(INT)
    for t in range(n_table):
        req[t] = wanted[t:t + 1, :]
    asked_ref[me_t] = req[me_t]

    @pl.loop(1, n_table)
    def _(i):
        peer = lax.rem(me_t + i, n_table)
        pltpu.make_async_remote_copy(
            src_ref=req.at[peer], dst_ref=asked_ref.at[me_t], send_sem=send_t.at[i], recv_sem=recv_t.at[me_t],
            device_id={"table": peer}, device_id_type=MESH).start()

    for copy in copies:
        copy.wait_send()

    @pl.loop(1, n_table)
    def _(i):
        peer = lax.rem(me_t + i, n_table)
        pltpu.make_async_remote_copy(
            src_ref=req.at[peer], dst_ref=asked_ref.at[peer], send_sem=send_t.at[i], recv_sem=recv_t.at[peer],
            device_id={"table": peer}, device_id_type=MESH).wait()


def route_call(n_dp, n_table, owners, rows, lengths, dest):
    seqs, events = rows.shape
    lines = events // 128
    vm = pl.BlockSpec(memory_space=pltpu.VMEM)
    sm = pl.BlockSpec(memory_space=pltpu.SMEM)
    return pl.pallas_call(
        functools.partial(route_kernel, seqs, n_dp, n_table),
        out_shape=(jax.ShapeDtypeStruct((n_table, 1, 128), INT), jax.ShapeDtypeStruct((seqs, lines, 128), INT)),
        in_specs=[vm, vm, sm, sm],
        out_specs=(vm, vm),
        scratch_shapes=[
            pltpu.VMEM((seqs * lines + 8, 128), INT),
            pltpu.VMEM((n_dp, seqs * lines + 8, 128), INT),
            pltpu.VMEM((n_table, 1, 128), INT),
            pltpu.SemaphoreType.DMA((n_dp,)),
            pltpu.SemaphoreType.DMA((n_dp,)),
            pltpu.SemaphoreType.DMA((n_table,)),
            pltpu.SemaphoreType.DMA((n_table,)),
        ],
        compiler_params=pltpu.CompilerParams(collective_id=0, has_side_effects=True),
        name="route",
    )(owners, rows, lengths, dest)


def on_device(owners, local_rows, lengths, destinations, table, gain_in, w_in, b_in, gain_out, w_out, b_out):
    seqs, events = local_rows.shape
    n_dp, n_table = lax.axis_size("dp"), lax.axis_size("table")
    asked, slot = route_call(n_dp, n_table, owners.reshape(seqs, events), local_rows, lengths, destinations)
    answers = []
    for s in range(seqs):
        wanted = asked[:, 0, s * SLOTS:(s + 1) * SLOTS].reshape(-1)
        found = jnp.take(table, wanted, axis=0, mode="clip").reshape(n_table, SLOTS, table.shape[1])
        answers.append(lax.all_to_all(found, "table", split_axis=0, concat_axis=0, tiled=True))
    out = None
    for s in range(seqs):
        out = layer_call(s, slot[s], answers[s].reshape(n_table * SLOTS, table.shape[1]),
                         gain_in, w_in, b_in, gain_out, w_out, b_out, out)
    return out


def solution(mesh):
    placed = (
        P(("dp", "table"), None, None),
        P(("dp", "table"), None),
        P(("dp", "table")),
        P("table", "dp"),
        P("table", None),
        P(),
        P(),
        P(),
        P(),
        P(),
        P(),
    )
    return jax.shard_map(
        on_device,
        mesh=mesh,
        in_specs=placed,
        out_specs=P(("dp", "table"), None, None),
        check_vma=False,
    )
```

```python
import functools
import jax
import jax.numpy as jnp
from jax import lax
from jax.experimental import pallas as pl
from jax.experimental.pallas import tpu as pltpu
from jax.sharding import PartitionSpec as P

HEADS = 8
EPS = 1e-05
BLK = 256
BF = jnp.bfloat16
F32 = jnp.float32


def silu_half(u):
    return u + u * jnp.tanh(u)


def norm_rows(values, gain):
    centre = jnp.mean(values, axis=-1, keepdims=True)
    spread = values - centre
    variance = jnp.mean(spread * spread, axis=-1, keepdims=True)
    return spread * lax.rsqrt(variance + EPS) * gain


def layer_kernel(slot_ref, rows_ref, gain_in_ref, w_in_ref, b_in_ref, gain_out_ref, w_out_ref, b_out_ref,
                 out_ref, hist, gate, q, k, v0, v1, att):
    events, width = hist.shape
    slots = rows_ref.shape[0]
    lanes = lax.broadcasted_iota(jnp.int32, (128, 128), 1)
    subs = lax.broadcasted_iota(jnp.int32, (128, 128), 0)
    eye = lanes == subs
    half = lax.broadcasted_iota(jnp.int32, (BLK, 128), 1) < 64

    def project(c, carry):
        cols = []
        for i in range(BLK // 128):
            line = slot_ref[pl.ds(c * (BLK // 128) + i, 1), :]
            spread = jnp.where(eye, jnp.broadcast_to(line, (128, 128)), 0)
            cols.append(jnp.sum(spread, axis=1, keepdims=True))
        col = jnp.concatenate(cols, axis=0)
        here = (col >= 0).astype(F32)
        pick = (col == lax.broadcasted_iota(jnp.int32, (BLK, slots), 1)).astype(F32).astype(BF)
        rows = jnp.dot(pick, rows_ref[...], preferred_element_type=F32)
        at = pl.ds(pl.multiple_of(c * BLK, BLK), BLK)
        hist[at, :] = rows.astype(BF)
        normed = norm_rows(rows, gain_in_ref[...]).astype(BF)
        for part in range(4):
            cs = slice(part * width, (part + 1) * width)
            pre = jnp.dot(normed, w_in_ref[:, cs], preferred_element_type=F32) + b_in_ref[:, cs]
            act = silu_half(0.5 * pre)
            if part == 0:
                gate[at, :] = act
            elif part == 1:
                act = act * here
                for p in range(4):
                    piece = act[:, p * 128:(p + 1) * 128]
                    v0[p, at, :] = jnp.where(half, piece, 0.0).astype(BF)
                    v1[p, at, :] = jnp.where(half, 0.0, piece).astype(BF)
            else:
                target = q if part == 2 else k
                act = act.astype(BF)
                for p in range(4):
                    target[p, at, :] = act[:, p * 128:(p + 1) * 128]
        return carry

    lax.fori_loop(0, events // BLK, project, 0)

    tri = lax.broadcasted_iota(jnp.int32, (BLK, BLK), 0) >= lax.broadcasted_iota(jnp.int32, (BLK, BLK), 1)

    def attend(p, carry):
        for i in range(events // BLK):
            at = slice(i * BLK, (i + 1) * BLK)
            qb = q[p, at, :] * jnp.bfloat16(0.0625)
            total = None
            for h, v in ((0, v0), (1, v1)):
                qh = jnp.where(half == (h == 0), qb.astype(F32), 0.0).astype(BF)
                for j in range(i + 1):
                    ks = slice(j * BLK, (j + 1) * BLK)
                    s = lax.dot_general(qh, k[p, ks, :], (((1,), (1,)), ((), ())), preferred_element_type=F32)
                    w = silu_half(s)
                    if j == i:
                        w = jnp.where(tri, w, 0.0)
                    o = jnp.dot(w.astype(BF), v[p, ks, :], preferred_element_type=F32)
                    total = o if total is None else total + o
            att[p, at, :] = total
        return carry

    lax.fori_loop(0, 4, attend, 0)

    def finish(c, carry):
        cols = []
        for i in range(BLK // 128):
            line = slot_ref[pl.ds(c * (BLK // 128) + i, 1), :]
            spread = jnp.where(eye, jnp.broadcast_to(line, (128, 128)), 0)
            cols.append(jnp.sum(spread, axis=1, keepdims=True))
        here = jnp.concatenate(cols, axis=0) >= 0
        at = pl.ds(pl.multiple_of(c * BLK, BLK), BLK)
        full = jnp.concatenate([att[p, at, :] for p in range(4)], axis=1)
        gated = (norm_rows(full, gain_out_ref[...]) * gate[at, :]).astype(BF)
        update = jnp.dot(gated, w_out_ref[...], preferred_element_type=F32) + b_out_ref[...]
        out_ref[0, at, :] = jnp.where(here, hist[at, :].astype(F32) + update, 0.0).astype(BF)
        return carry

    lax.fori_loop(0, events // BLK, finish, 0)


def layer_call(s, slot, rows, gain_in, w_in, b_in, gain_out, w_out, b_out, before):
    events = slot.shape[0] * 128
    width = rows.shape[1]
    vm = pl.BlockSpec(memory_space=pltpu.VMEM)
    ins = [slot, rows, gain_in[None], w_in, b_in[None], gain_out[None], w_out, b_out[None]]
    specs = [vm] * len(ins)
    kernel = layer_kernel
    aliases = {}
    if before is not None:
        ins.append(before)
        specs.append(pl.BlockSpec(memory_space=pl.ANY))
        aliases = {len(ins) - 1: 0}

        def kernel(*refs):
            layer_kernel(*refs[:8], *refs[9:])
    return pl.pallas_call(
        kernel,
        grid=(1,),
        in_specs=specs,
        out_specs=pl.BlockSpec((1, events, width), lambda i: (s, 0, 0)),
        out_shape=jax.ShapeDtypeStruct((2, events, width), BF),
        scratch_shapes=[
            pltpu.VMEM((events, width), BF),
            pltpu.VMEM((events, width), F32),
            pltpu.VMEM((4, events, 128), BF),
            pltpu.VMEM((4, events, 128), BF),
            pltpu.VMEM((4, events, 128), BF),
            pltpu.VMEM((4, events, 128), BF),
            pltpu.VMEM((4, events, 128), F32),
        ],
        input_output_aliases=aliases,
        compiler_params=pltpu.CompilerParams(vmem_limit_bytes=40 << 20),
        cost_estimate=pl.CostEstimate(flops=8 * 10**9, bytes_accessed=8 << 20, transcendentals=8 << 20),
        name="layer",
    )(*ins)
MESH = pl.DeviceIdType.MESH
SLOTS = 48
INT = jnp.int32


def route_kernel(seqs, n_dp, n_table, owners_ref, rows_ref, lengths_ref, dest_ref, table_ref, slot_ref, answer_ref,
                 mine, every, req, asked, wanted_rows, wide, picked, parcel, send_z, recv_z, send_t, recv_t, fetch_sem,
                 send_rows, recv_rows):
    me_dp, me_t = lax.axis_index("dp"), lax.axis_index("table")
    events = owners_ref.shape[1]
    lines = events // 128
    barrier = pltpu.get_barrier_semaphore()
    for i in range(1, n_dp):
        pl.semaphore_signal(barrier, inc=1, device_id={"dp": lax.rem(me_dp + i, n_dp)}, device_id_type=MESH)

    @pl.loop(1, n_table)
    def _(i):
        pl.semaphore_signal(barrier, inc=1, device_id={"table": lax.rem(me_t + i, n_table)}, device_id_type=MESH)

    lane = lax.broadcasted_iota(INT, (1, 128), 1)
    for s in range(seqs):
        for r in range(lines):
            cs = slice(r * 128, (r + 1) * 128)
            packed = owners_ref[s:s + 1, cs] * 4096 + rows_ref[s:s + 1, cs]
            mine[s * lines + r:s * lines + r + 1, :] = jnp.where(lane + r * 128 < lengths_ref[s], packed, -1)
    for j in range(8):
        mine[seqs * lines + j:seqs * lines + j + 1, :] = jnp.zeros((1, 128), INT) + dest_ref[0, min(j, seqs - 1)]
    every[me_dp] = mine[...]
    pl.semaphore_wait(barrier, n_dp - 1 + n_table - 1)

    copies = []
    for i in range(1, n_dp):
        copy = pltpu.make_async_remote_copy(
            src_ref=mine, dst_ref=every.at[me_dp], send_sem=send_z.at[i], recv_sem=recv_z.at[me_dp],
            device_id={"dp": lax.rem(me_dp + i, n_dp)}, device_id_type=MESH)
        copy.start()
        copies.append(copy)
    @pl.loop(0, table_ref.shape[0] // 64)
    def _(i):
        at = pl.ds(pl.multiple_of(i * 64, 64), 64)
        wide[at, :] = table_ref[at, :].astype(F32)

    for i in range(1, n_dp):
        pltpu.make_async_remote_copy(
            src_ref=mine, dst_ref=every.at[lax.rem(me_dp + i, n_dp)], send_sem=send_z.at[i],
            recv_sem=recv_z.at[lax.rem(me_dp + i, n_dp)],
            device_id={"dp": lax.rem(me_dp + i, n_dp)}, device_id_type=MESH).wait_recv()

    shard = lax.broadcasted_iota(INT, (n_table, 128), 0)
    place = lax.broadcasted_iota(INT, (128, 128), 0)
    upper = (place <= lax.broadcasted_iota(INT, (128, 128), 1)).astype(F32).astype(BF)
    request = jnp.zeros((2 * n_table, 128), F32)
    for s in range(seqs):
        refs = jnp.zeros((lines, 128), INT)
        for d in range(n_dp):
            for j in range(seqs):
                went = every[d, seqs * lines + j:seqs * lines + j + 1, :]
                refs += jnp.where(went == me_dp * seqs + s, every[d, j * lines:(j + 1) * lines, :], 0)
        owner, row = refs >> 12, refs & 4095
        named = [(jnp.broadcast_to(owner[r:r + 1, :], (n_table, 128)) == shard) for r in range(lines)]
        before = jnp.zeros((n_table, 1), F32)
        for r in range(lines):
            hot = named[r].astype(F32)
            upto = jnp.dot(hot.astype(BF), upper, preferred_element_type=F32) + before
            before += jnp.sum(hot, axis=1, keepdims=True)
            rank = jnp.sum(jnp.where(named[r], upto - 1.0, 0.0), axis=0, keepdims=True)
            slot = jnp.sum(jnp.where(named[r], upto + (shard * SLOTS).astype(F32), 0.0), axis=0, keepdims=True)
            slot_ref[s, r:r + 1, :] = slot.astype(INT) - 1
            high = jnp.broadcast_to(row[r:r + 1, :] >> 6, (n_table, 128)).astype(F32)
            low = jnp.broadcast_to(row[r:r + 1, :] & 63, (n_table, 128)).astype(F32)
            left = jnp.concatenate([jnp.where(named[r], high, 0.0), jnp.where(named[r], low, 0.0)], axis=0)
            right = jnp.broadcast_to(rank.astype(INT) + s * SLOTS, (128, 128)) == place
            request += lax.dot_general(left.astype(BF), right.astype(F32).astype(BF), (((1,), (1,)), ((), ())),
                                       preferred_element_type=F32)
    wanted = (request[:n_table] * 64.0 + request[n_table:]).astype(INT)
    for t in range(n_table):
        req[t] = wanted[t:t + 1, :]
    asked[me_t] = req[me_t]

    @pl.loop(1, n_table)
    def _(i):
        peer = lax.rem(me_t + i, n_table)
        pltpu.make_async_remote_copy(
            src_ref=req.at[peer], dst_ref=asked.at[me_t], send_sem=send_t.at[i], recv_sem=recv_t.at[me_t],
            device_id={"table": peer}, device_id_type=MESH).start()

    for copy in copies:
        copy.wait_send()

    @pl.loop(1, n_table)
    def _(i):
        peer = lax.rem(me_t + i, n_table)
        pltpu.make_async_remote_copy(
            src_ref=req.at[peer], dst_ref=asked.at[peer], send_sem=send_t.at[i], recv_sem=recv_t.at[peer],
            device_id={"table": peer}, device_id_type=MESH).wait()

    fetch = pltpu.make_async_copy(asked, wanted_rows, fetch_sem)
    fetch.start()
    fetch.wait()

    def pick(s, peer):
        for k in range(SLOTS):
            picked[k:k + 1, :] = wide[pl.ds(wanted_rows[peer, 0, s * SLOTS + k] & (wide.shape[0] - 1), 1), :]

    def row_copy(s, i, peer, other):
        return pltpu.make_async_remote_copy(
            src_ref=parcel.at[s, peer], dst_ref=answer_ref.at[s, other], send_sem=send_rows.at[s, i],
            recv_sem=recv_rows.at[s, other], device_id={"table": peer}, device_id_type=MESH)

    for s in range(seqs):
        @pl.loop(1, n_table)
        def _(i):
            peer = lax.rem(me_t + i, n_table)
            pick(s, peer)
            parcel[s, peer] = picked[...].astype(BF)
            row_copy(s, i, peer, me_t).start()

        pick(s, me_t)
        answer_ref[s, me_t] = picked[...].astype(BF)

    for s in range(seqs):
        @pl.loop(1, n_table)
        def _(i):
            peer = lax.rem(me_t + i, n_table)
            row_copy(s, i, peer, peer).wait()


def route_call(n_dp, n_table, owners, rows, lengths, dest, table):
    seqs, events = rows.shape
    lines = events // 128
    vm = pl.BlockSpec(memory_space=pltpu.VMEM)
    sm = pl.BlockSpec(memory_space=pltpu.SMEM)
    return pl.pallas_call(
        functools.partial(route_kernel, seqs, n_dp, n_table),
        out_shape=(jax.ShapeDtypeStruct((seqs, lines, 128), INT),
                   jax.ShapeDtypeStruct((seqs, n_table, SLOTS, table.shape[1]), BF)),
        in_specs=[vm, vm, sm, sm, vm],
        out_specs=(vm, vm),
        scratch_shapes=[
            pltpu.VMEM((seqs * lines + 8, 128), INT),
            pltpu.VMEM((n_dp, seqs * lines + 8, 128), INT),
            pltpu.VMEM((n_table, 1, 128), INT),
            pltpu.VMEM((n_table, 1, 128), INT),
            pltpu.SMEM((n_table, 1, 128), INT),
            pltpu.VMEM(table.shape, F32),
            pltpu.VMEM((SLOTS, table.shape[1]), F32),
            pltpu.VMEM((seqs, n_table, SLOTS, table.shape[1]), BF),
            pltpu.SemaphoreType.DMA((n_dp,)),
            pltpu.SemaphoreType.DMA((n_dp,)),
            pltpu.SemaphoreType.DMA((n_table,)),
            pltpu.SemaphoreType.DMA((n_table,)),
            pltpu.SemaphoreType.DMA,
            pltpu.SemaphoreType.DMA((seqs, n_table)),
            pltpu.SemaphoreType.DMA((seqs, n_table)),
        ],
        compiler_params=pltpu.CompilerParams(collective_id=0, has_side_effects=True, vmem_limit_bytes=40 << 20),
        name="route",
    )(owners, rows, lengths, dest, table)


def on_device(owners, local_rows, lengths, destinations, table, gain_in, w_in, b_in, gain_out, w_out, b_out):
    seqs, events = local_rows.shape
    n_dp, n_table = lax.axis_size("dp"), lax.axis_size("table")
    slot, answers = route_call(
        n_dp, n_table, owners.reshape(seqs, events), local_rows, lengths, destinations, table)
    out = None
    for s in range(seqs):
        out = layer_call(s, slot[s], answers[s].reshape(n_table * SLOTS, table.shape[1]),
                         gain_in, w_in, b_in, gain_out, w_out, b_out, out)
    return out


def solution(mesh):
    placed = (
        P(("dp", "table"), None, None),
        P(("dp", "table"), None),
        P(("dp", "table")),
        P("table", "dp"),
        P("table", None),
        P(),
        P(),
        P(),
        P(),
        P(),
        P(),
    )
    return jax.shard_map(
        on_device,
        mesh=mesh,
        in_specs=placed,
        out_specs=P(("dp", "table"), None, None),
        check_vma=False,
    )
```

```python
import functools
import jax
import jax.numpy as jnp
from jax import lax
from jax.experimental import pallas as pl
from jax.experimental.pallas import tpu as pltpu
from jax.sharding import PartitionSpec as P

HEADS = 8
EPS = 1e-05
BLK = 256
BF = jnp.bfloat16
F32 = jnp.float32
INT = jnp.int32
MESH = pl.DeviceIdType.MESH
SLOTS = 48


def silu_half(u):
    return u + u * jnp.tanh(u)


def norm_rows(values, gain):
    centre = jnp.mean(values, axis=-1, keepdims=True)
    spread = values - centre
    variance = jnp.mean(spread * spread, axis=-1, keepdims=True)
    return spread * lax.rsqrt(variance + EPS) * gain


def layer_body(slot_ref, rows_ref, weights, out_ref, done, hist, gate, q, k, v0, v1, att):
    gain_in_ref, w_in_ref, b_in_ref, gain_out_ref, w_out_ref, b_out_ref = weights
    events, width = hist.shape
    slots = rows_ref.shape[0]
    lanes = lax.broadcasted_iota(jnp.int32, (128, 128), 1)
    subs = lax.broadcasted_iota(jnp.int32, (128, 128), 0)
    eye = lanes == subs
    half = lax.broadcasted_iota(jnp.int32, (BLK, 128), 1) < 64

    def project(c, carry):
        cols = []
        for i in range(BLK // 128):
            line = slot_ref[pl.ds(c * (BLK // 128) + i, 1), :]
            spread = jnp.where(eye, jnp.broadcast_to(line, (128, 128)), 0)
            cols.append(jnp.sum(spread, axis=1, keepdims=True))
        col = jnp.concatenate(cols, axis=0)
        here = (col >= 0).astype(F32)
        pick = (col == lax.broadcasted_iota(jnp.int32, (BLK, slots), 1)).astype(F32).astype(BF)
        rows = jnp.dot(pick, rows_ref[...], preferred_element_type=F32)
        at = pl.ds(pl.multiple_of(c * BLK, BLK), BLK)
        hist[at, :] = rows.astype(BF)
        normed = norm_rows(rows, gain_in_ref[...]).astype(BF)
        for part in range(4):
            cs = slice(part * width, (part + 1) * width)
            pre = jnp.dot(normed, w_in_ref[:, cs], preferred_element_type=F32) + b_in_ref[:, cs]
            act = silu_half(0.5 * pre)
            if part == 0:
                gate[at, :] = act
            elif part == 1:
                act = act * here
                for p in range(4):
                    piece = act[:, p * 128:(p + 1) * 128]
                    v0[p, at, :] = jnp.where(half, piece, 0.0).astype(BF)
                    v1[p, at, :] = jnp.where(half, 0.0, piece).astype(BF)
            else:
                target = q if part == 2 else k
                act = act.astype(BF)
                for p in range(4):
                    target[p, at, :] = act[:, p * 128:(p + 1) * 128]
        return carry

    lax.fori_loop(0, events // BLK, project, 0)

    tri = lax.broadcasted_iota(jnp.int32, (BLK, BLK), 0) >= lax.broadcasted_iota(jnp.int32, (BLK, BLK), 1)

    def attend(p, carry):
        for i in range(events // BLK):
            at = slice(i * BLK, (i + 1) * BLK)
            qb = q[p, at, :] * jnp.bfloat16(0.0625)
            total = None
            for h, v in ((0, v0), (1, v1)):
                qh = jnp.where(half == (h == 0), qb.astype(F32), 0.0).astype(BF)
                for j in range(i + 1):
                    ks = slice(j * BLK, (j + 1) * BLK)
                    s = lax.dot_general(qh, k[p, ks, :], (((1,), (1,)), ((), ())), preferred_element_type=F32)
                    w = silu_half(s)
                    if j == i:
                        w = jnp.where(tri, w, 0.0)
                    o = jnp.dot(w.astype(BF), v[p, ks, :], preferred_element_type=F32)
                    total = o if total is None else total + o
            att[p, at, :] = total
        return carry

    lax.fori_loop(0, 4, attend, 0)

    def finish(c, carry):
        cols = []
        for i in range(BLK // 128):
            line = slot_ref[pl.ds(c * (BLK // 128) + i, 1), :]
            spread = jnp.where(eye, jnp.broadcast_to(line, (128, 128)), 0)
            cols.append(jnp.sum(spread, axis=1, keepdims=True))
        here = jnp.concatenate(cols, axis=0) >= 0
        at = pl.ds(pl.multiple_of(c * BLK, BLK), BLK)
        full = jnp.concatenate([att[p, at, :] for p in range(4)], axis=1)
        gated = (norm_rows(full, gain_out_ref[...]) * gate[at, :]).astype(BF)
        update = jnp.dot(gated, w_out_ref[...], preferred_element_type=F32) + b_out_ref[...]
        out_ref[at, :] = jnp.where(here, hist[at, :].astype(F32) + update, 0.0).astype(BF)
        done(c, at)
        return carry

    lax.fori_loop(0, events // BLK, finish, 0)


def layer_scratch(events):
    return [
        pltpu.VMEM((events, 512), BF),
        pltpu.VMEM((events, 512), F32),
        pltpu.VMEM((4, events, 128), BF),
        pltpu.VMEM((4, events, 128), BF),
        pltpu.VMEM((4, events, 128), BF),
        pltpu.VMEM((4, events, 128), BF),
        pltpu.VMEM((4, events, 128), F32),
    ]


def weight_scratch(weights):
    return [pltpu.VMEM(w.shape, w.dtype) for w in weights] + [pltpu.SemaphoreType.DMA((len(weights),))]


def fetch_kernel(seqs, n_dp, n_table, owners_hbm, rows_hbm, lengths_hbm, dest_hbm, table_hbm, *refs):
    weights_hbm, refs = refs[:6], refs[6:]
    slot_ref, later_ref, out_ref = refs[:3]
    (owners, rows, lengths, dest, table, local_sem), refs = refs[3:9], refs[9:]
    weights, weight_sem, refs = refs[:6], refs[6], refs[7:]
    (mine, every, req, asked, wanted_rows, wide, picked, parcel, first,
     send_z, recv_z, send_t, recv_t, fetch_sem, send_rows, recv_rows), work = refs[:16], refs[16:]
    me_dp, me_t = lax.axis_index("dp"), lax.axis_index("table")
    events = rows.shape[1]
    lines = events // 128

    inputs = [(owners_hbm, owners), (rows_hbm, rows), (lengths_hbm, lengths), (dest_hbm, dest), (table_hbm, table)]
    local = [pltpu.make_async_copy(a, b, local_sem.at[i]) for i, (a, b) in enumerate(inputs)]
    local += [pltpu.make_async_copy(a, b, weight_sem.at[i]) for i, (a, b) in enumerate(zip(weights_hbm, weights))]
    for copy in local:
        copy.start()

    barrier = pltpu.get_barrier_semaphore()
    for i in range(1, n_dp):
        pl.semaphore_signal(barrier, inc=1, device_id={"dp": lax.rem(me_dp + i, n_dp)}, device_id_type=MESH)

    @pl.loop(1, n_table)
    def _(i):
        pl.semaphore_signal(barrier, inc=1, device_id={"table": lax.rem(me_t + i, n_table)}, device_id_type=MESH)

    for copy in local[:4]:
        copy.wait()
    lane = lax.broadcasted_iota(INT, (1, 128), 1)
    for s in range(seqs):
        for r in range(lines):
            cs = slice(r * 128, (r + 1) * 128)
            packed = owners[s, :, cs] * 4096 + rows[s:s + 1, cs]
            mine[s * lines + r:s * lines + r + 1, :] = jnp.where(lane + r * 128 < lengths[s], packed, -1)
    for j in range(8):
        mine[seqs * lines + j:seqs * lines + j + 1, :] = jnp.zeros((1, 128), INT) + dest[0, min(j, seqs - 1)]
    every[me_dp] = mine[...]
    pl.semaphore_wait(barrier, n_dp - 1 + n_table - 1)

    copies = []
    for i in range(1, n_dp):
        copy = pltpu.make_async_remote_copy(
            src_ref=mine, dst_ref=every.at[me_dp], send_sem=send_z.at[i], recv_sem=recv_z.at[me_dp],
            device_id={"dp": lax.rem(me_dp + i, n_dp)}, device_id_type=MESH)
        copy.start()
        copies.append(copy)
    def widen(begin, end):
        @pl.loop(begin, end)
        def _(i):
            at = pl.ds(pl.multiple_of(i * 64, 64), 64)
            wide[at, :] = table[at, :].astype(F32)

    chunks = table.shape[0] // 64
    local[4].wait()
    widen(0, chunks // 2)
    for i in range(1, n_dp):
        pltpu.make_async_remote_copy(
            src_ref=mine, dst_ref=every.at[lax.rem(me_dp + i, n_dp)], send_sem=send_z.at[i],
            recv_sem=recv_z.at[lax.rem(me_dp + i, n_dp)],
            device_id={"dp": lax.rem(me_dp + i, n_dp)}, device_id_type=MESH).wait_recv()

    shard = lax.broadcasted_iota(INT, (n_table, 128), 0)
    place = lax.broadcasted_iota(INT, (128, 128), 0)
    upper = (place <= lax.broadcasted_iota(INT, (128, 128), 1)).astype(F32).astype(BF)
    request = jnp.zeros((2 * n_table, 128), F32)
    for s in range(seqs):
        refs = jnp.zeros((lines, 128), INT)
        for d in range(n_dp):
            for j in range(seqs):
                went = every[d, seqs * lines + j:seqs * lines + j + 1, :]
                refs += jnp.where(went == me_dp * seqs + s, every[d, j * lines:(j + 1) * lines, :], 0)
        owner, row = refs >> 12, refs & 4095
        named = [(jnp.broadcast_to(owner[r:r + 1, :], (n_table, 128)) == shard) for r in range(lines)]
        before = jnp.zeros((n_table, 1), F32)
        for r in range(lines):
            hot = named[r].astype(F32)
            upto = jnp.dot(hot.astype(BF), upper, preferred_element_type=F32) + before
            before += jnp.sum(hot, axis=1, keepdims=True)
            rank = jnp.sum(jnp.where(named[r], upto - 1.0, 0.0), axis=0, keepdims=True)
            slot = jnp.sum(jnp.where(named[r], upto + (shard * SLOTS).astype(F32), 0.0), axis=0, keepdims=True)
            slot_ref[s, r:r + 1, :] = slot.astype(INT) - 1
            high = jnp.broadcast_to(row[r:r + 1, :] >> 6, (n_table, 128)).astype(F32)
            low = jnp.broadcast_to(row[r:r + 1, :] & 63, (n_table, 128)).astype(F32)
            left = jnp.concatenate([jnp.where(named[r], high, 0.0), jnp.where(named[r], low, 0.0)], axis=0)
            right = jnp.broadcast_to(rank.astype(INT) + s * SLOTS, (128, 128)) == place
            request += lax.dot_general(left.astype(BF), right.astype(F32).astype(BF), (((1,), (1,)), ((), ())),
                                       preferred_element_type=F32)
    wanted = (request[:n_table] * 64.0 + request[n_table:]).astype(INT)
    for t in range(n_table):
        req[t] = wanted[t:t + 1, :]
    asked[me_t] = req[me_t]

    @pl.loop(1, n_table)
    def _(i):
        peer = lax.rem(me_t + i, n_table)
        pltpu.make_async_remote_copy(
            src_ref=req.at[peer], dst_ref=asked.at[me_t], send_sem=send_t.at[i], recv_sem=recv_t.at[me_t],
            device_id={"table": peer}, device_id_type=MESH).start()

    widen(chunks // 2, chunks)
    for copy in copies:
        copy.wait_send()

    @pl.loop(1, n_table)
    def _(i):
        peer = lax.rem(me_t + i, n_table)
        pltpu.make_async_remote_copy(
            src_ref=req.at[peer], dst_ref=asked.at[peer], send_sem=send_t.at[i], recv_sem=recv_t.at[peer],
            device_id={"table": peer}, device_id_type=MESH).wait()

    fetch = pltpu.make_async_copy(asked, wanted_rows, fetch_sem)
    fetch.start()
    fetch.wait()

    def part(t):
        return pl.ds(pl.multiple_of(t * SLOTS, SLOTS), SLOTS)

    def pick(s, peer):
        for k in range(SLOTS):
            row = wanted_rows[peer, 0, s * SLOTS + k] & (wide.shape[0] - 1)
            picked[k:k + 1, :] = wide[pl.ds(row, 1), :]

    def row_copy(s, i, peer, other):
        return pltpu.make_async_remote_copy(
            src_ref=parcel.at[s, peer], dst_ref=(first, later_ref)[s].at[part(other)], send_sem=send_rows.at[s, i],
            recv_sem=recv_rows.at[s, other], device_id={"table": peer}, device_id_type=MESH)

    for s in range(seqs):
        @pl.loop(1, n_table)
        def _(i):
            peer = lax.rem(me_t + i, n_table)
            pick(s, peer)
            parcel[s, peer] = picked[...].astype(BF)
            row_copy(s, i, peer, me_t).start()

        pick(s, me_t)
        (first, later_ref)[s][part(me_t), :] = picked[...].astype(BF)

    for copy in local[5:]:
        copy.wait()

    def settle(s):
        @pl.loop(1, n_table)
        def _(i):
            peer = lax.rem(me_t + i, n_table)
            row_copy(s, i, peer, peer).wait()

    settle(0)
    layer_body(slot_ref.at[0], first, weights, out_ref, lambda c, at: None, *work)
    settle(1)


def fetch_call(n_dp, n_table, owners, rows, lengths, dest, table, weights):
    seqs, events = rows.shape
    lines, width = events // 128, table.shape[1]
    any_space = pl.BlockSpec(memory_space=pl.ANY)
    vm = pl.BlockSpec(memory_space=pltpu.VMEM)
    return pl.pallas_call(
        functools.partial(fetch_kernel, seqs, n_dp, n_table),
        out_shape=(jax.ShapeDtypeStruct((seqs, lines, 128), INT),
                   jax.ShapeDtypeStruct((n_table * SLOTS, width), BF),
                   jax.ShapeDtypeStruct((events, width), BF)),
        in_specs=[any_space] * (5 + len(weights)),
        out_specs=(vm, vm, vm),
        scratch_shapes=[
            pltpu.VMEM(owners.shape, INT),
            pltpu.VMEM(rows.shape, INT),
            pltpu.SMEM(lengths.shape, INT),
            pltpu.SMEM(dest.shape, INT),
            pltpu.VMEM(table.shape, BF),
            pltpu.SemaphoreType.DMA((5,)),
            *weight_scratch(weights),
            pltpu.VMEM((seqs * lines + 8, 128), INT),
            pltpu.VMEM((n_dp, seqs * lines + 8, 128), INT),
            pltpu.VMEM((n_table, 1, 128), INT),
            pltpu.VMEM((n_table, 1, 128), INT),
            pltpu.SMEM((n_table, 1, 128), INT),
            pltpu.VMEM(table.shape, F32),
            pltpu.VMEM((SLOTS, width), F32),
            pltpu.VMEM((seqs, n_table, SLOTS, width), BF),
            pltpu.VMEM((n_table * SLOTS, width), BF),
            pltpu.SemaphoreType.DMA((n_dp,)),
            pltpu.SemaphoreType.DMA((n_dp,)),
            pltpu.SemaphoreType.DMA((n_table,)),
            pltpu.SemaphoreType.DMA((n_table,)),
            pltpu.SemaphoreType.DMA,
            pltpu.SemaphoreType.DMA((seqs, n_table)),
            pltpu.SemaphoreType.DMA((seqs, n_table)),
            *layer_scratch(events),
        ],
        compiler_params=pltpu.CompilerParams(collective_id=0, has_side_effects=True, vmem_limit_bytes=60 << 20),
        name="fetch",
    )(owners, rows, lengths, dest, table, *weights)


def last_kernel(slot_ref, rows_ref, ready_ref, *refs):
    weights_hbm, out_hbm, refs = refs[:6], refs[6], refs[7:]
    weights, weight_sem, refs = refs[:6], refs[6], refs[7:]
    out, ready_sem, out_sem, work = refs[0], refs[1], refs[2], refs[3:]
    local = [pltpu.make_async_copy(a, b, weight_sem.at[i]) for i, (a, b) in enumerate(zip(weights_hbm, weights))]
    for copy in local:
        copy.start()
    ready = pltpu.make_async_copy(ready_ref, out_hbm.at[0], ready_sem)
    ready.start()
    for copy in local:
        copy.wait()

    def send(c, at):
        pltpu.make_async_copy(out.at[at], out_hbm.at[1, at], out_sem.at[c]).start()

    layer_body(slot_ref.at[1], rows_ref, weights, out, send, *work)
    for c in range(out.shape[0] // BLK):
        at = pl.ds(c * BLK, BLK)
        pltpu.make_async_copy(out.at[at], out_hbm.at[1, at], out_sem.at[c]).wait()
    ready.wait()


def last_call(slot, rows, ready, weights):
    events, width = ready.shape
    any_space = pl.BlockSpec(memory_space=pl.ANY)
    vm = pl.BlockSpec(memory_space=pltpu.VMEM)
    return pl.pallas_call(
        last_kernel,
        out_shape=jax.ShapeDtypeStruct((2, events, width), BF),
        in_specs=[vm, vm, vm] + [any_space] * len(weights),
        out_specs=any_space,
        scratch_shapes=[
            *weight_scratch(weights),
            pltpu.VMEM((events, width), BF),
            pltpu.SemaphoreType.DMA,
            pltpu.SemaphoreType.DMA((events // BLK,)),
            *layer_scratch(events),
        ],
        compiler_params=pltpu.CompilerParams(vmem_limit_bytes=60 << 20),
        name="last",
    )(slot, rows, ready, *weights)


def on_device(owners, local_rows, lengths, destinations, table, gain_in, w_in, b_in, gain_out, w_out, b_out):
    seqs, events = local_rows.shape
    n_dp, n_table = lax.axis_size("dp"), lax.axis_size("table")
    weights = (gain_in[None], w_in, b_in[None], gain_out[None], w_out, b_out[None])
    slot, rows, ready = fetch_call(
        n_dp, n_table, owners.reshape(seqs, 1, events), local_rows, lengths, destinations, table, weights)
    return last_call(slot, rows, ready, weights)


def solution(mesh):
    placed = (
        P(("dp", "table"), None, None),
        P(("dp", "table"), None),
        P(("dp", "table")),
        P("table", "dp"),
        P("table", None),
        P(),
        P(),
        P(),
        P(),
        P(),
        P(),
    )
    return jax.shard_map(
        on_device,
        mesh=mesh,
        in_specs=placed,
        out_specs=P(("dp", "table"), None, None),
        check_vma=False,
    )
```

```python
import functools
import jax
import jax.numpy as jnp
from jax import lax
from jax.experimental import pallas as pl
from jax.experimental.pallas import tpu as pltpu
from jax.sharding import PartitionSpec as P

HEADS = 8
EPS = 1e-05
BLK = 256
BF = jnp.bfloat16
F32 = jnp.float32
INT = jnp.int32
MESH = pl.DeviceIdType.MESH
SLOTS = 48


def silu_half(u):
    return u + u * jnp.tanh(u)


def norm_rows(values, gain):
    centre = jnp.mean(values, axis=-1, keepdims=True)
    spread = values - centre
    variance = jnp.mean(spread * spread, axis=-1, keepdims=True)
    return spread * lax.rsqrt(variance + EPS) * gain


def layer_body(slot_ref, rows_ref, weights, out_ref, done, hist, gate, q, k, v0, v1, att):
    gain_in_ref, w_in_ref, b_in_ref, gain_out_ref, w_out_ref, b_out_ref = weights
    events, width = hist.shape
    slots = rows_ref.shape[0]
    lanes = lax.broadcasted_iota(jnp.int32, (128, 128), 1)
    subs = lax.broadcasted_iota(jnp.int32, (128, 128), 0)
    eye = lanes == subs
    half = lax.broadcasted_iota(jnp.int32, (BLK, 128), 1) < 64

    def project(c, carry):
        cols = []
        for i in range(BLK // 128):
            line = slot_ref[pl.ds(c * (BLK // 128) + i, 1), :]
            spread = jnp.where(eye, jnp.broadcast_to(line, (128, 128)), 0)
            cols.append(jnp.sum(spread, axis=1, keepdims=True))
        col = jnp.concatenate(cols, axis=0)
        here = (col >= 0).astype(F32)
        pick = (col == lax.broadcasted_iota(jnp.int32, (BLK, slots), 1)).astype(F32).astype(BF)
        rows = jnp.dot(pick, rows_ref[...], preferred_element_type=F32)
        at = pl.ds(pl.multiple_of(c * BLK, BLK), BLK)
        hist[at, :] = rows.astype(BF)
        normed = norm_rows(rows, gain_in_ref[...]).astype(BF)
        for part in range(4):
            cs = slice(part * width, (part + 1) * width)
            pre = jnp.dot(normed, w_in_ref[:, cs], preferred_element_type=F32) + b_in_ref[:, cs]
            act = silu_half(0.5 * pre)
            if part == 0:
                gate[at, :] = act
            elif part == 1:
                act = act * here
                for p in range(4):
                    piece = act[:, p * 128:(p + 1) * 128]
                    v0[p, at, :] = jnp.where(half, piece, 0.0).astype(BF)
                    v1[p, at, :] = jnp.where(half, 0.0, piece).astype(BF)
            else:
                target = q if part == 2 else k
                act = act.astype(BF)
                for p in range(4):
                    target[p, at, :] = act[:, p * 128:(p + 1) * 128]
        return carry

    lax.fori_loop(0, events // BLK, project, 0)

    tri = lax.broadcasted_iota(jnp.int32, (BLK, BLK), 0) >= lax.broadcasted_iota(jnp.int32, (BLK, BLK), 1)

    def attend(p, carry):
        for i in range(events // BLK):
            at = slice(i * BLK, (i + 1) * BLK)
            qb = q[p, at, :] * jnp.bfloat16(0.0625)
            total = None
            for h, v in ((0, v0), (1, v1)):
                qh = jnp.where(half == (h == 0), qb.astype(F32), 0.0).astype(BF)
                for j in range(i + 1):
                    ks = slice(j * BLK, (j + 1) * BLK)
                    s = lax.dot_general(qh, k[p, ks, :], (((1,), (1,)), ((), ())), preferred_element_type=F32)
                    w = silu_half(s)
                    if j == i:
                        w = jnp.where(tri, w, 0.0)
                    o = jnp.dot(w.astype(BF), v[p, ks, :], preferred_element_type=F32)
                    total = o if total is None else total + o
            att[p, at, :] = total
        return carry

    lax.fori_loop(0, 4, attend, 0)

    def finish(c, carry):
        cols = []
        for i in range(BLK // 128):
            line = slot_ref[pl.ds(c * (BLK // 128) + i, 1), :]
            spread = jnp.where(eye, jnp.broadcast_to(line, (128, 128)), 0)
            cols.append(jnp.sum(spread, axis=1, keepdims=True))
        here = jnp.concatenate(cols, axis=0) >= 0
        at = pl.ds(pl.multiple_of(c * BLK, BLK), BLK)
        full = jnp.concatenate([att[p, at, :] for p in range(4)], axis=1)
        gated = (norm_rows(full, gain_out_ref[...]) * gate[at, :]).astype(BF)
        update = jnp.dot(gated, w_out_ref[...], preferred_element_type=F32) + b_out_ref[...]
        out_ref[at, :] = jnp.where(here, hist[at, :].astype(F32) + update, 0.0).astype(BF)
        done(c, at)
        return carry

    lax.fori_loop(0, events // BLK, finish, 0)


def layer_scratch(events):
    return [
        pltpu.VMEM((events, 512), BF),
        pltpu.VMEM((events, 512), F32),
        pltpu.VMEM((4, events, 128), BF),
        pltpu.VMEM((4, events, 128), BF),
        pltpu.VMEM((4, events, 128), BF),
        pltpu.VMEM((4, events, 128), BF),
        pltpu.VMEM((4, events, 128), F32),
    ]


def weight_scratch(weights):
    return [pltpu.VMEM(w.shape, w.dtype) for w in weights] + [pltpu.SemaphoreType.DMA((len(weights),))]


def fetch_kernel(seqs, n_dp, n_table, owners_hbm, rows_hbm, lengths_hbm, dest_hbm, table_hbm, *refs):
    weights_hbm, refs = refs[:6], refs[6:]
    slot_ref, later_ref, out_ref = refs[:3]
    (owners, rows, lengths, dest, table, local_sem), refs = refs[3:9], refs[9:]
    weights, weight_sem, refs = refs[:6], refs[6], refs[7:]
    (mine, every, req, asked, wanted_rows, wide, picked, parcel, first,
     send_z, recv_z, send_t, recv_t, fetch_sem, send_rows, recv_rows,
     relay, relay_in, relay_out), work = refs[:19], refs[19:]
    me_dp, me_t = lax.axis_index("dp"), lax.axis_index("table")
    events = rows.shape[1]
    lines = events // 128

    inputs = [(owners_hbm, owners), (rows_hbm, rows), (lengths_hbm, lengths), (dest_hbm, dest), (table_hbm, table)]
    local = [pltpu.make_async_copy(a, b, local_sem.at[i]) for i, (a, b) in enumerate(inputs)]
    local += [pltpu.make_async_copy(a, b, weight_sem.at[i]) for i, (a, b) in enumerate(zip(weights_hbm, weights))]
    for copy in local:
        copy.start()

    barrier = pltpu.get_barrier_semaphore()
    for i in range(1, n_dp):
        pl.semaphore_signal(barrier, inc=1, device_id={"dp": lax.rem(me_dp + i, n_dp)}, device_id_type=MESH)

    @pl.loop(1, n_table)
    def _(i):
        pl.semaphore_signal(barrier, inc=1, device_id={"table": lax.rem(me_t + i, n_table)}, device_id_type=MESH)

    for copy in local[:4]:
        copy.wait()
    lane = lax.broadcasted_iota(INT, (1, 128), 1)
    for s in range(seqs):
        for r in range(lines):
            cs = slice(r * 128, (r + 1) * 128)
            packed = owners[s, :, cs] * 4096 + rows[s:s + 1, cs]
            mine[s * lines + r:s * lines + r + 1, :] = jnp.where(lane + r * 128 < lengths[s], packed, -1)
    for j in range(8):
        mine[seqs * lines + j:seqs * lines + j + 1, :] = jnp.zeros((1, 128), INT) + dest[0, min(j, seqs - 1)]
    every[me_dp] = mine[...]
    pl.semaphore_wait(barrier, n_dp - 1 + n_table - 1)

    copies = []
    for i in range(1, n_dp):
        copy = pltpu.make_async_remote_copy(
            src_ref=mine, dst_ref=every.at[me_dp], send_sem=send_z.at[i], recv_sem=recv_z.at[me_dp],
            device_id={"dp": lax.rem(me_dp + i, n_dp)}, device_id_type=MESH)
        copy.start()
        copies.append(copy)
    def widen(begin, end):
        @pl.loop(begin, end)
        def _(i):
            at = pl.ds(pl.multiple_of(i * 64, 64), 64)
            wide[at, :] = table[at, :].astype(F32)

    chunks = table.shape[0] // 64
    local[4].wait()
    widen(0, chunks // 2)
    for i in range(1, n_dp):
        pltpu.make_async_remote_copy(
            src_ref=mine, dst_ref=every.at[lax.rem(me_dp + i, n_dp)], send_sem=send_z.at[i],
            recv_sem=recv_z.at[lax.rem(me_dp + i, n_dp)],
            device_id={"dp": lax.rem(me_dp + i, n_dp)}, device_id_type=MESH).wait_recv()

    shard = lax.broadcasted_iota(INT, (n_table, 128), 0)
    place = lax.broadcasted_iota(INT, (128, 128), 0)
    upper = (place <= lax.broadcasted_iota(INT, (128, 128), 1)).astype(F32).astype(BF)
    request = jnp.zeros((2 * n_table, 128), F32)
    for s in range(seqs):
        refs = jnp.zeros((lines, 128), INT)
        for d in range(n_dp):
            for j in range(seqs):
                went = every[d, seqs * lines + j:seqs * lines + j + 1, :]
                refs += jnp.where(went == me_dp * seqs + s, every[d, j * lines:(j + 1) * lines, :], 0)
        owner, row = refs >> 12, refs & 4095
        named = [(jnp.broadcast_to(owner[r:r + 1, :], (n_table, 128)) == shard) for r in range(lines)]
        before = jnp.zeros((n_table, 1), F32)
        for r in range(lines):
            hot = named[r].astype(F32)
            upto = jnp.dot(hot.astype(BF), upper, preferred_element_type=F32) + before
            before += jnp.sum(hot, axis=1, keepdims=True)
            rank = jnp.sum(jnp.where(named[r], upto - 1.0, 0.0), axis=0, keepdims=True)
            slot = jnp.sum(jnp.where(named[r], upto + (shard * SLOTS).astype(F32), 0.0), axis=0, keepdims=True)
            slot_ref[s, r:r + 1, :] = slot.astype(INT) - 1
            high = jnp.broadcast_to(row[r:r + 1, :] >> 6, (n_table, 128)).astype(F32)
            low = jnp.broadcast_to(row[r:r + 1, :] & 63, (n_table, 128)).astype(F32)
            left = jnp.concatenate([jnp.where(named[r], high, 0.0), jnp.where(named[r], low, 0.0)], axis=0)
            right = jnp.broadcast_to(rank.astype(INT) + s * SLOTS, (128, 128)) == place
            request += lax.dot_general(left.astype(BF), right.astype(F32).astype(BF), (((1,), (1,)), ((), ())),
                                       preferred_element_type=F32)
    wanted = (request[:n_table] * 64.0 + request[n_table:]).astype(INT)
    for t in range(n_table):
        req[t] = wanted[t:t + 1, :]
    asked[me_t] = req[me_t]

    @pl.loop(1, n_table)
    def _(i):
        peer = lax.rem(me_t + i, n_table)
        pltpu.make_async_remote_copy(
            src_ref=req.at[peer], dst_ref=asked.at[me_t], send_sem=send_t.at[i], recv_sem=recv_t.at[me_t],
            device_id={"table": peer}, device_id_type=MESH).start()

    widen(chunks // 2, chunks)
    for copy in copies:
        copy.wait_send()

    @pl.loop(1, n_table)
    def _(i):
        peer = lax.rem(me_t + i, n_table)
        pltpu.make_async_remote_copy(
            src_ref=req.at[peer], dst_ref=asked.at[peer], send_sem=send_t.at[i], recv_sem=recv_t.at[peer],
            device_id={"table": peer}, device_id_type=MESH).wait()

    fetch = pltpu.make_async_copy(asked, wanted_rows, fetch_sem)
    fetch.start()
    fetch.wait()

    def part(t):
        return pl.ds(pl.multiple_of(t * SLOTS, SLOTS), SLOTS)

    def pick(s, peer):
        for k in range(SLOTS):
            row = wanted_rows[peer, 0, s * SLOTS + k] & (wide.shape[0] - 1)
            picked[k:k + 1, :] = wide[pl.ds(row, 1), :]

    y0, x0, c0 = me_t // 8, me_t // 2 % 4, me_t % 2

    def at_offset(dy, dx, dc):
        return (y0 + dy) % 4 * 8 + (x0 + dx) % 4 * 2 + (c0 + dc) % 2

    def detour(j):
        late = j // 4
        dy = (1 - late) * 2 + late * ((j + 4) % 4 + j // 6)
        dx = (1 - late) * (j % 4) + late * 2
        return dy, dx, dy // 2 * (3 - dy) * 3, dx // 2 * (3 - dx) * 3

    def straight(k):
        late = k // 15
        m = (k + 9) % 24 % 9
        dy = (1 - late) * ((k + 1) // 4) + late * (m // 3 + m // 6)
        dx = (1 - late) * ((k + 1) % 4) + late * (m % 3 + m % 3 // 2)
        return dy, dx, late

    landing = (first, later_ref)

    def send_straight(s, k):
        dy, dx, dc = straight(k)
        peer = at_offset(dy, dx, dc)
        return peer, pltpu.make_async_remote_copy(
            src_ref=parcel.at[s, peer], dst_ref=landing[s].at[part(me_t)], send_sem=send_rows.at[s, peer],
            recv_sem=recv_rows.at[s, me_t], device_id={"table": peer}, device_id_type=MESH)

    def send_halfway(s, j):
        dy, dx, hy, hx = detour(j)
        peer = at_offset(dy, dx, 1)
        return peer, pltpu.make_async_remote_copy(
            src_ref=parcel.at[s, peer], dst_ref=relay.at[s, j], send_sem=send_rows.at[s, peer],
            recv_sem=relay_in.at[s, j], device_id={"table": at_offset(hy, hx, 0)}, device_id_type=MESH)

    def send_on(s, j):
        dy, dx, hy, hx = detour(j)
        origin = at_offset(4 - hy, 4 - hx, 0)
        return pltpu.make_async_remote_copy(
            src_ref=relay.at[s, j], dst_ref=landing[s].at[part(origin)], send_sem=relay_out.at[s, j],
            recv_sem=recv_rows.at[s, origin], device_id={"table": at_offset(4 + dy - hy, 4 + dx - hx, 1)},
            device_id_type=MESH)

    def load(s, peer):
        pick(s, peer)
        parcel[s, peer] = picked[...].astype(BF)

    def all_halfway(s):
        @pl.loop(0, 7)
        def _(j):
            peer, copy = send_halfway(s, j)
            load(s, peer)
            copy.start()

    def all_straight(s):
        @pl.loop(0, 24)
        def _(k):
            peer, copy = send_straight(s, k)
            load(s, peer)
            copy.start()

    def all_on(s):
        @pl.loop(0, 7)
        def _(j):
            send_halfway(s, j)[1].wait_recv()
            send_on(s, j).start()

    all_halfway(0)
    all_straight(0)
    all_halfway(1)
    all_on(0)
    all_straight(1)
    for s in range(seqs):
        pick(s, me_t)
        landing[s][part(me_t), :] = picked[...].astype(BF)
    all_on(1)
    for copy in local[5:]:
        copy.wait()

    def settle(s):
        @pl.loop(0, 24)
        def _(k):
            dy, dx, dc = straight(k)
            source = at_offset(4 - dy, 4 - dx, dc)
            pltpu.make_async_remote_copy(
                src_ref=parcel.at[s, source], dst_ref=landing[s].at[part(source)], send_sem=send_rows.at[s, source],
                recv_sem=recv_rows.at[s, source], device_id={"table": source}, device_id_type=MESH).wait_recv()

        @pl.loop(0, 7)
        def _(j):
            dy, dx, hy, hx = detour(j)
            source = at_offset(4 - dy, 4 - dx, 1)
            pltpu.make_async_remote_copy(
                src_ref=parcel.at[s, source], dst_ref=landing[s].at[part(source)], send_sem=send_rows.at[s, source],
                recv_sem=recv_rows.at[s, source], device_id={"table": source}, device_id_type=MESH).wait_recv()

    def sent(s):
        @pl.loop(0, 24)
        def _(k):
            send_straight(s, k)[1].wait_send()

        @pl.loop(0, 7)
        def _(j):
            send_halfway(s, j)[1].wait_send()
            send_on(s, j).wait_send()

    settle(0)
    layer_body(slot_ref.at[0], first, weights, out_ref, lambda c, at: None, *work)
    settle(1)
    sent(0)
    sent(1)


def fetch_call(n_dp, n_table, owners, rows, lengths, dest, table, weights):
    seqs, events = rows.shape
    lines, width = events // 128, table.shape[1]
    any_space = pl.BlockSpec(memory_space=pl.ANY)
    vm = pl.BlockSpec(memory_space=pltpu.VMEM)
    return pl.pallas_call(
        functools.partial(fetch_kernel, seqs, n_dp, n_table),
        out_shape=(jax.ShapeDtypeStruct((seqs, lines, 128), INT),
                   jax.ShapeDtypeStruct((n_table * SLOTS, width), BF),
                   jax.ShapeDtypeStruct((events, width), BF)),
        in_specs=[any_space] * (5 + len(weights)),
        out_specs=(vm, vm, vm),
        scratch_shapes=[
            pltpu.VMEM(owners.shape, INT),
            pltpu.VMEM(rows.shape, INT),
            pltpu.SMEM(lengths.shape, INT),
            pltpu.SMEM(dest.shape, INT),
            pltpu.VMEM(table.shape, BF),
            pltpu.SemaphoreType.DMA((5,)),
            *weight_scratch(weights),
            pltpu.VMEM((seqs * lines + 8, 128), INT),
            pltpu.VMEM((n_dp, seqs * lines + 8, 128), INT),
            pltpu.VMEM((n_table, 1, 128), INT),
            pltpu.VMEM((n_table, 1, 128), INT),
            pltpu.SMEM((n_table, 1, 128), INT),
            pltpu.VMEM(table.shape, F32),
            pltpu.VMEM((SLOTS, width), F32),
            pltpu.VMEM((seqs, n_table, SLOTS, width), BF),
            pltpu.VMEM((n_table * SLOTS, width), BF),
            pltpu.SemaphoreType.DMA((n_dp,)),
            pltpu.SemaphoreType.DMA((n_dp,)),
            pltpu.SemaphoreType.DMA((n_table,)),
            pltpu.SemaphoreType.DMA((n_table,)),
            pltpu.SemaphoreType.DMA,
            pltpu.SemaphoreType.DMA((seqs, n_table)),
            pltpu.SemaphoreType.DMA((seqs, n_table)),
            pltpu.VMEM((seqs, 7, SLOTS, width), BF),
            pltpu.SemaphoreType.DMA((seqs, 7)),
            pltpu.SemaphoreType.DMA((seqs, 7)),
            *layer_scratch(events),
        ],
        compiler_params=pltpu.CompilerParams(collective_id=0, has_side_effects=True, vmem_limit_bytes=60 << 20),
        name="fetch",
    )(owners, rows, lengths, dest, table, *weights)


def last_kernel(slot_ref, rows_ref, ready_ref, *refs):
    weights_hbm, out_hbm, refs = refs[:6], refs[6], refs[7:]
    weights, weight_sem, refs = refs[:6], refs[6], refs[7:]
    out, ready_sem, out_sem, work = refs[0], refs[1], refs[2], refs[3:]
    local = [pltpu.make_async_copy(a, b, weight_sem.at[i]) for i, (a, b) in enumerate(zip(weights_hbm, weights))]
    for copy in local:
        copy.start()
    ready = pltpu.make_async_copy(ready_ref, out_hbm.at[0], ready_sem)
    ready.start()
    for copy in local:
        copy.wait()

    def send(c, at):
        pltpu.make_async_copy(out.at[at], out_hbm.at[1, at], out_sem.at[c]).start()

    layer_body(slot_ref.at[1], rows_ref, weights, out, send, *work)
    for c in range(out.shape[0] // BLK):
        at = pl.ds(c * BLK, BLK)
        pltpu.make_async_copy(out.at[at], out_hbm.at[1, at], out_sem.at[c]).wait()
    ready.wait()


def last_call(slot, rows, ready, weights):
    events, width = ready.shape
    any_space = pl.BlockSpec(memory_space=pl.ANY)
    vm = pl.BlockSpec(memory_space=pltpu.VMEM)
    return pl.pallas_call(
        last_kernel,
        out_shape=jax.ShapeDtypeStruct((2, events, width), BF),
        in_specs=[vm, vm, vm] + [any_space] * len(weights),
        out_specs=any_space,
        scratch_shapes=[
            *weight_scratch(weights),
            pltpu.VMEM((events, width), BF),
            pltpu.SemaphoreType.DMA,
            pltpu.SemaphoreType.DMA((events // BLK,)),
            *layer_scratch(events),
        ],
        compiler_params=pltpu.CompilerParams(vmem_limit_bytes=60 << 20),
        name="last",
    )(slot, rows, ready, *weights)


def on_device(owners, local_rows, lengths, destinations, table, gain_in, w_in, b_in, gain_out, w_out, b_out):
    seqs, events = local_rows.shape
    n_dp, n_table = lax.axis_size("dp"), lax.axis_size("table")
    weights = (gain_in[None], w_in, b_in[None], gain_out[None], w_out, b_out[None])
    slot, rows, ready = fetch_call(
        n_dp, n_table, owners.reshape(seqs, 1, events), local_rows, lengths, destinations, table, weights)
    return last_call(slot, rows, ready, weights)


def solution(mesh):
    placed = (
        P(("dp", "table"), None, None),
        P(("dp", "table"), None),
        P(("dp", "table")),
        P("table", "dp"),
        P("table", None),
        P(),
        P(),
        P(),
        P(),
        P(),
        P(),
    )
    return jax.shard_map(
        on_device,
        mesh=mesh,
        in_specs=placed,
        out_specs=P(("dp", "table"), None, None),
        check_vma=False,
    )
```

```python
import functools
import jax
import jax.numpy as jnp
from jax import lax
from jax.experimental import pallas as pl
from jax.experimental.pallas import tpu as pltpu
from jax.sharding import PartitionSpec as P

HEADS = 8
EPS = 1e-05
BLK = 256
BF = jnp.bfloat16
F32 = jnp.float32
INT = jnp.int32
MESH = pl.DeviceIdType.MESH
SLOTS = 48


def silu_half(u):
    return u + u * jnp.tanh(u)


def norm_rows(values, gain):
    centre = jnp.mean(values, axis=-1, keepdims=True)
    spread = values - centre
    variance = jnp.mean(spread * spread, axis=-1, keepdims=True)
    return spread * lax.rsqrt(variance + EPS) * gain


def layer_body(slot_ref, rows_ref, weights, out_ref, done, hist, gate, q, k, v0, v1, att):
    gain_in_ref, w_in_ref, b_in_ref, gain_out_ref, w_out_ref, b_out_ref = weights
    events, width = hist.shape
    slots = rows_ref.shape[0]
    lanes = lax.broadcasted_iota(jnp.int32, (128, 128), 1)
    subs = lax.broadcasted_iota(jnp.int32, (128, 128), 0)
    eye = lanes == subs
    half = lax.broadcasted_iota(jnp.int32, (BLK, 128), 1) < 64

    def project(c, carry):
        cols = []
        for i in range(BLK // 128):
            line = slot_ref[pl.ds(c * (BLK // 128) + i, 1), :]
            spread = jnp.where(eye, jnp.broadcast_to(line, (128, 128)), 0)
            cols.append(jnp.sum(spread, axis=1, keepdims=True))
        col = jnp.concatenate(cols, axis=0)
        here = (col >= 0).astype(F32)
        pick = (col == lax.broadcasted_iota(jnp.int32, (BLK, slots), 1)).astype(F32).astype(BF)
        rows = jnp.dot(pick, rows_ref[...], preferred_element_type=F32)
        at = pl.ds(pl.multiple_of(c * BLK, BLK), BLK)
        hist[at, :] = rows.astype(BF)
        normed = norm_rows(rows, gain_in_ref[...] * 0.5).astype(BF)
        for part in range(4):
            cs = slice(part * width, (part + 1) * width)
            pre = jnp.dot(normed, w_in_ref[:, cs], preferred_element_type=F32) + b_in_ref[:, cs] * 0.5
            act = silu_half(pre)
            if part == 0:
                gate[at, :] = act
            elif part == 1:
                act = act * here
                for p in range(4):
                    piece = act[:, p * 128:(p + 1) * 128]
                    v0[p, at, :] = jnp.where(half, piece, 0.0).astype(BF)
                    v1[p, at, :] = jnp.where(half, 0.0, piece).astype(BF)
            else:
                for p in range(4):
                    piece = act[:, p * 128:(p + 1) * 128]
                    if part == 3:
                        k[p, at, :] = piece.astype(BF)
                    else:
                        piece = piece * 0.0625
                        q[2 * p, at, :] = jnp.where(half, piece, 0.0).astype(BF)
                        q[2 * p + 1, at, :] = jnp.where(half, 0.0, piece).astype(BF)
        return carry

    lax.fori_loop(0, events // BLK, project, 0, unroll=True)

    tri = lax.broadcasted_iota(jnp.int32, (BLK, BLK), 0) >= lax.broadcasted_iota(jnp.int32, (BLK, BLK), 1)

    def attend(p, carry):
        for j in range(events // BLK):
            ks = slice(j * BLK, (j + 1) * BLK)
            rest = slice(j * BLK, events)
            for h, v in ((0, v0), (1, v1)):
                s = lax.dot_general(q[2 * p + h, rest, :], k[p, ks, :], (((1,), (1,)), ((), ())), preferred_element_type=F32)
                w = silu_half(s)
                head = jnp.where(tri, w[:BLK], 0.0).astype(BF)
                w = jnp.concatenate([head, w[BLK:].astype(BF)], axis=0) if j < events // BLK - 1 else head
                o = jnp.dot(w, v[p, ks, :], preferred_element_type=F32)
                if j == 0 and h == 0:
                    att[p, rest, :] = o
                else:
                    att[p, rest, :] += o
        return carry

    lax.fori_loop(0, 4, attend, 0)

    def finish(c, carry):
        cols = []
        for i in range(BLK // 128):
            line = slot_ref[pl.ds(c * (BLK // 128) + i, 1), :]
            spread = jnp.where(eye, jnp.broadcast_to(line, (128, 128)), 0)
            cols.append(jnp.sum(spread, axis=1, keepdims=True))
        here = jnp.concatenate(cols, axis=0) >= 0
        at = pl.ds(pl.multiple_of(c * BLK, BLK), BLK)
        full = jnp.concatenate([att[p, at, :] for p in range(4)], axis=1)
        gated = (norm_rows(full, gain_out_ref[...]) * gate[at, :]).astype(BF)
        update = jnp.dot(gated, w_out_ref[...], preferred_element_type=F32) + b_out_ref[...]
        out_ref[at, :] = jnp.where(here, hist[at, :].astype(F32) + update, 0.0).astype(BF)
        done(c, at)
        return carry

    lax.fori_loop(0, events // BLK, finish, 0, unroll=True)


def layer_scratch(events):
    return [
        pltpu.VMEM((events, 512), BF),
        pltpu.VMEM((events, 512), F32),
        pltpu.VMEM((8, events, 128), BF),
        pltpu.VMEM((4, events, 128), BF),
        pltpu.VMEM((4, events, 128), BF),
        pltpu.VMEM((4, events, 128), BF),
        pltpu.VMEM((4, events, 128), F32),
    ]


def weight_scratch(weights):
    return [pltpu.VMEM(w.shape, w.dtype) for w in weights] + [pltpu.SemaphoreType.DMA((len(weights),))]


def fetch_kernel(seqs, n_dp, n_table, owners_hbm, rows_hbm, lengths_hbm, dest_hbm, table_hbm, *refs):
    weights_hbm, refs = refs[:6], refs[6:]
    slot_ref, later_ref, out_ref = refs[:3]
    (owners, rows, lengths, dest, table, local_sem), refs = refs[3:9], refs[9:]
    weights, weight_sem, refs = refs[:6], refs[6], refs[7:]
    (mine, every, req, asked, wanted_rows, wide, picked, parcel, first,
     send_z, recv_z, send_t, recv_t, fetch_sem, send_rows, recv_rows), work = refs[:16], refs[16:]
    me_dp, me_t = lax.axis_index("dp"), lax.axis_index("table")
    events = rows.shape[1]
    lines = events // 128

    inputs = [(owners_hbm, owners), (rows_hbm, rows), (lengths_hbm, lengths), (dest_hbm, dest), (table_hbm, table)]
    local = [pltpu.make_async_copy(a, b, local_sem.at[i]) for i, (a, b) in enumerate(inputs)]
    local += [pltpu.make_async_copy(a, b, weight_sem.at[i]) for i, (a, b) in enumerate(zip(weights_hbm, weights))]
    for copy in local:
        copy.start()

    barrier = pltpu.get_barrier_semaphore()
    for i in range(1, n_dp):
        pl.semaphore_signal(barrier, inc=1, device_id={"dp": lax.rem(me_dp + i, n_dp)}, device_id_type=MESH)

    @pl.loop(1, n_table)
    def _(i):
        pl.semaphore_signal(barrier, inc=1, device_id={"table": lax.rem(me_t + i, n_table)}, device_id_type=MESH)

    for copy in local[:4]:
        copy.wait()
    lane = lax.broadcasted_iota(INT, (1, 128), 1)
    for s in range(seqs):
        for r in range(lines):
            cs = slice(r * 128, (r + 1) * 128)
            packed = owners[s, :, cs] * 4096 + rows[s:s + 1, cs]
            mine[s * lines + r:s * lines + r + 1, :] = jnp.where(lane + r * 128 < lengths[s], packed, -1)
    for j in range(8):
        mine[seqs * lines + j:seqs * lines + j + 1, :] = jnp.zeros((1, 128), INT) + dest[0, min(j, seqs - 1)]
    every[me_dp] = mine[...]
    pl.semaphore_wait(barrier, n_dp - 1 + n_table - 1)

    copies = []
    for i in range(1, n_dp):
        copy = pltpu.make_async_remote_copy(
            src_ref=mine, dst_ref=every.at[me_dp], send_sem=send_z.at[i], recv_sem=recv_z.at[me_dp],
            device_id={"dp": lax.rem(me_dp + i, n_dp)}, device_id_type=MESH)
        copy.start()
        copies.append(copy)
    def widen(begin, end):
        @pl.loop(begin, end)
        def _(i):
            at = pl.ds(pl.multiple_of(i * 64, 64), 64)
            wide[at, :] = table[at, :].astype(F32)

    chunks = table.shape[0] // 64
    local[4].wait()
    widen(0, chunks // 2)
    for i in range(1, n_dp):
        pltpu.make_async_remote_copy(
            src_ref=mine, dst_ref=every.at[lax.rem(me_dp + i, n_dp)], send_sem=send_z.at[i],
            recv_sem=recv_z.at[lax.rem(me_dp + i, n_dp)],
            device_id={"dp": lax.rem(me_dp + i, n_dp)}, device_id_type=MESH).wait_recv()

    shard = lax.broadcasted_iota(INT, (n_table, 128), 0)
    place = lax.broadcasted_iota(INT, (128, 128), 0)
    upper = (place <= lax.broadcasted_iota(INT, (128, 128), 1)).astype(F32).astype(BF)
    request = jnp.zeros((2 * n_table, 128), F32)
    for s in range(seqs):
        refs = jnp.zeros((lines, 128), INT)
        for d in range(n_dp):
            for j in range(seqs):
                went = every[d, seqs * lines + j:seqs * lines + j + 1, :]
                refs += jnp.where(went == me_dp * seqs + s, every[d, j * lines:(j + 1) * lines, :], 0)
        owner, row = refs >> 12, refs & 4095
        named = [(jnp.broadcast_to(owner[r:r + 1, :], (n_table, 128)) == shard) for r in range(lines)]
        before = jnp.zeros((n_table, 1), F32)
        for r in range(lines):
            hot = named[r].astype(F32)
            upto = jnp.dot(hot.astype(BF), upper, preferred_element_type=F32) + before
            before += jnp.sum(hot, axis=1, keepdims=True)
            rank = jnp.sum(jnp.where(named[r], upto - 1.0, 0.0), axis=0, keepdims=True)
            slot = jnp.sum(jnp.where(named[r], upto + (shard * SLOTS).astype(F32), 0.0), axis=0, keepdims=True)
            slot_ref[s, r:r + 1, :] = slot.astype(INT) - 1
            high = jnp.broadcast_to(row[r:r + 1, :] >> 6, (n_table, 128)).astype(F32)
            low = jnp.broadcast_to(row[r:r + 1, :] & 63, (n_table, 128)).astype(F32)
            left = jnp.concatenate([jnp.where(named[r], high, 0.0), jnp.where(named[r], low, 0.0)], axis=0)
            right = jnp.broadcast_to(rank.astype(INT) + s * SLOTS, (128, 128)) == place
            request += lax.dot_general(left.astype(BF), right.astype(F32).astype(BF), (((1,), (1,)), ((), ())),
                                       preferred_element_type=F32)
    wanted = (request[:n_table] * 64.0 + request[n_table:]).astype(INT)
    for t in range(n_table):
        req[t] = wanted[t:t + 1, :]
    asked[me_t] = req[me_t]

    @pl.loop(1, n_table)
    def _(i):
        peer = lax.rem(me_t + i, n_table)
        pltpu.make_async_remote_copy(
            src_ref=req.at[peer], dst_ref=asked.at[me_t], send_sem=send_t.at[i], recv_sem=recv_t.at[me_t],
            device_id={"table": peer}, device_id_type=MESH).start()

    widen(chunks // 2, chunks)
    for copy in copies:
        copy.wait_send()

    @pl.loop(1, n_table)
    def _(i):
        peer = lax.rem(me_t + i, n_table)
        pltpu.make_async_remote_copy(
            src_ref=req.at[peer], dst_ref=asked.at[peer], send_sem=send_t.at[i], recv_sem=recv_t.at[peer],
            device_id={"table": peer}, device_id_type=MESH).wait()

    fetch = pltpu.make_async_copy(asked, wanted_rows, fetch_sem)
    fetch.start()
    fetch.wait()

    def part(t):
        return pl.ds(pl.multiple_of(t * SLOTS, SLOTS), SLOTS)

    def pick(s, peer):
        for k in range(SLOTS):
            row = wanted_rows[peer, 0, s * SLOTS + k] & (wide.shape[0] - 1)
            picked[k:k + 1, :] = wide[pl.ds(row, 1), :]

    def row_copy(s, i, peer, other):
        return pltpu.make_async_remote_copy(
            src_ref=parcel.at[s, peer], dst_ref=(first, later_ref)[s].at[part(other)], send_sem=send_rows.at[s, i],
            recv_sem=recv_rows.at[s, other], device_id={"table": peer}, device_id_type=MESH)

    turn = lax.rem(me_t * 7, n_table - 1)
    y0, x0, c0 = me_t // 8, me_t // 2 % 4, me_t % 2

    for s in range(seqs):
        @pl.loop(0, n_table - 1)
        def _(k):
            i = lax.rem(k + turn, n_table - 1) + 1
            peer = (y0 + i // 8) % 4 * 8 + (x0 + i // 2 % 4) % 4 * 2 + (c0 + i % 2) % 2
            pick(s, peer)
            parcel[s, peer] = picked[...].astype(BF)
            row_copy(s, peer, peer, me_t).start()

        pick(s, me_t)
        (first, later_ref)[s][part(me_t), :] = picked[...].astype(BF)

    for copy in local[5:]:
        copy.wait()

    def settle(s):
        @pl.loop(1, n_table)
        def _(i):
            peer = lax.rem(me_t + i, n_table)
            row_copy(s, peer, peer, peer).wait()

    settle(0)
    layer_body(slot_ref.at[0], first, weights, out_ref, lambda c, at: None, *work)
    settle(1)


def fetch_call(n_dp, n_table, owners, rows, lengths, dest, table, weights):
    seqs, events = rows.shape
    lines, width = events // 128, table.shape[1]
    any_space = pl.BlockSpec(memory_space=pl.ANY)
    vm = pl.BlockSpec(memory_space=pltpu.VMEM)
    return pl.pallas_call(
        functools.partial(fetch_kernel, seqs, n_dp, n_table),
        out_shape=(jax.ShapeDtypeStruct((seqs, lines, 128), INT),
                   jax.ShapeDtypeStruct((n_table * SLOTS, width), BF),
                   jax.ShapeDtypeStruct((events, width), BF)),
        in_specs=[any_space] * (5 + len(weights)),
        out_specs=(vm, vm, vm),
        scratch_shapes=[
            pltpu.VMEM(owners.shape, INT),
            pltpu.VMEM(rows.shape, INT),
            pltpu.SMEM(lengths.shape, INT),
            pltpu.SMEM(dest.shape, INT),
            pltpu.VMEM(table.shape, BF),
            pltpu.SemaphoreType.DMA((5,)),
            *weight_scratch(weights),
            pltpu.VMEM((seqs * lines + 8, 128), INT),
            pltpu.VMEM((n_dp, seqs * lines + 8, 128), INT),
            pltpu.VMEM((n_table, 1, 128), INT),
            pltpu.VMEM((n_table, 1, 128), INT),
            pltpu.SMEM((n_table, 1, 128), INT),
            pltpu.VMEM(table.shape, F32),
            pltpu.VMEM((SLOTS, width), F32),
            pltpu.VMEM((seqs, n_table, SLOTS, width), BF),
            pltpu.VMEM((n_table * SLOTS, width), BF),
            pltpu.SemaphoreType.DMA((n_dp,)),
            pltpu.SemaphoreType.DMA((n_dp,)),
            pltpu.SemaphoreType.DMA((n_table,)),
            pltpu.SemaphoreType.DMA((n_table,)),
            pltpu.SemaphoreType.DMA,
            pltpu.SemaphoreType.DMA((seqs, n_table)),
            pltpu.SemaphoreType.DMA((seqs, n_table)),
            *layer_scratch(events),
        ],
        compiler_params=pltpu.CompilerParams(collective_id=0, has_side_effects=True, vmem_limit_bytes=60 << 20),
        name="fetch",
    )(owners, rows, lengths, dest, table, *weights)


def last_kernel(slot_ref, rows_ref, ready_ref, *refs):
    weights_hbm, out_hbm, refs = refs[:6], refs[6], refs[7:]
    weights, weight_sem, refs = refs[:6], refs[6], refs[7:]
    out, ready_sem, out_sem, work = refs[0], refs[1], refs[2], refs[3:]
    local = [pltpu.make_async_copy(a, b, weight_sem.at[i]) for i, (a, b) in enumerate(zip(weights_hbm, weights))]
    for copy in local:
        copy.start()
    ready = pltpu.make_async_copy(ready_ref, out_hbm.at[0], ready_sem)
    ready.start()
    for copy in local:
        copy.wait()

    def send(c, at):
        pltpu.make_async_copy(out.at[at], out_hbm.at[1, at], out_sem.at[c]).start()

    layer_body(slot_ref.at[1], rows_ref, weights, out, send, *work)
    for c in range(out.shape[0] // BLK):
        at = pl.ds(c * BLK, BLK)
        pltpu.make_async_copy(out.at[at], out_hbm.at[1, at], out_sem.at[c]).wait()
    ready.wait()


def last_call(slot, rows, ready, weights):
    events, width = ready.shape
    any_space = pl.BlockSpec(memory_space=pl.ANY)
    vm = pl.BlockSpec(memory_space=pltpu.VMEM)
    return pl.pallas_call(
        last_kernel,
        out_shape=jax.ShapeDtypeStruct((2, events, width), BF),
        in_specs=[vm, vm, vm] + [any_space] * len(weights),
        out_specs=any_space,
        scratch_shapes=[
            *weight_scratch(weights),
            pltpu.VMEM((events, width), BF),
            pltpu.SemaphoreType.DMA,
            pltpu.SemaphoreType.DMA((events // BLK,)),
            *layer_scratch(events),
        ],
        compiler_params=pltpu.CompilerParams(vmem_limit_bytes=60 << 20),
        name="last",
    )(slot, rows, ready, *weights)


def on_device(owners, local_rows, lengths, destinations, table, gain_in, w_in, b_in, gain_out, w_out, b_out):
    seqs, events = local_rows.shape
    n_dp, n_table = lax.axis_size("dp"), lax.axis_size("table")
    weights = (gain_in[None], w_in, b_in[None], gain_out[None], w_out, b_out[None])
    slot, rows, ready = fetch_call(
        n_dp, n_table, owners.reshape(seqs, 1, events), local_rows, lengths, destinations, table, weights)
    return last_call(slot, rows, ready, weights)


def solution(mesh):
    placed = (
        P(("dp", "table"), None, None),
        P(("dp", "table"), None),
        P(("dp", "table")),
        P("table", "dp"),
        P("table", None),
        P(),
        P(),
        P(),
        P(),
        P(),
        P(),
    )
    return jax.shard_map(
        on_device,
        mesh=mesh,
        in_specs=placed,
        out_specs=P(("dp", "table"), None, None),
        check_vma=False,
    )
```

```python
import functools
import jax
import jax.numpy as jnp
from jax import lax
from jax.experimental import pallas as pl
from jax.experimental.pallas import tpu as pltpu
from jax.sharding import PartitionSpec as P

HEADS = 8
EPS = 1e-05
BLK = 256
BF = jnp.bfloat16
F32 = jnp.float32
INT = jnp.int32
MESH = pl.DeviceIdType.MESH
SLOTS = 48


def silu_half(u):
    return u + u * jnp.tanh(u)


def norm_rows(values, gain):
    centre = jnp.mean(values, axis=-1, keepdims=True)
    spread = values - centre
    variance = jnp.mean(spread * spread, axis=-1, keepdims=True)
    return spread * lax.rsqrt(variance + EPS) * gain


def layer_body(slot_ref, rows_ref, weights, out_ref, done, hist, gate, q, k, v, att):
    gain_in_ref, w_in_ref, b_in_ref, gain_out_ref, w_out_ref, b_out_ref = weights
    events, width = hist.shape
    slots = rows_ref.shape[0]
    lanes = lax.broadcasted_iota(jnp.int32, (128, 128), 1)
    subs = lax.broadcasted_iota(jnp.int32, (128, 128), 0)
    eye = lanes == subs
    half = lax.broadcasted_iota(jnp.int32, (BLK, 128), 1) < 64

    def project(c, carry):
        cols = []
        for i in range(BLK // 128):
            line = slot_ref[pl.ds(c * (BLK // 128) + i, 1), :]
            spread = jnp.where(eye, jnp.broadcast_to(line, (128, 128)), 0)
            cols.append(jnp.sum(spread, axis=1, keepdims=True))
        col = jnp.concatenate(cols, axis=0)
        here = (col >= 0).astype(F32)
        pick = (col == lax.broadcasted_iota(jnp.int32, (BLK, slots), 1)).astype(F32).astype(BF)
        rows = jnp.dot(pick, rows_ref[...], preferred_element_type=F32)
        at = pl.ds(pl.multiple_of(c * BLK, BLK), BLK)
        hist[at, :] = rows.astype(BF)
        normed = norm_rows(rows, gain_in_ref[...] * 0.5).astype(BF)
        for part in range(4):
            cs = slice(part * width, (part + 1) * width)
            pre = jnp.dot(normed, w_in_ref[:, cs], preferred_element_type=F32) + b_in_ref[:, cs] * 0.5
            act = silu_half(pre)
            if part == 0:
                gate[at, :] = act
            elif part == 1:
                act = act * here
                for p in range(4):
                    piece = act[:, p * 128:(p + 1) * 128]
                    v[p, c, :BLK, :] = jnp.where(half, piece, 0.0).astype(BF)
                    v[p, c, BLK:, :] = jnp.where(half, 0.0, piece).astype(BF)
            else:
                for p in range(4):
                    piece = act[:, p * 128:(p + 1) * 128]
                    if part == 3:
                        k[p, at, :] = piece.astype(BF)
                    else:
                        piece = piece * 0.0625
                        q[2 * p, at, :] = jnp.where(half, piece, 0.0).astype(BF)
                        q[2 * p + 1, at, :] = jnp.where(half, 0.0, piece).astype(BF)
        return carry

    lax.fori_loop(0, events // BLK, project, 0, unroll=True)

    tri = lax.broadcasted_iota(jnp.int32, (BLK, BLK), 0) >= lax.broadcasted_iota(jnp.int32, (BLK, BLK), 1)

    def attend(p, carry):
        for j in range(events // BLK):
            ks = slice(j * BLK, (j + 1) * BLK)
            rest = slice(j * BLK, events)
            both = []
            for h in range(2):
                s = lax.dot_general(q[2 * p + h, rest, :], k[p, ks, :], (((1,), (1,)), ((), ())), preferred_element_type=F32)
                w = silu_half(s)
                head = jnp.where(tri, w[:BLK], 0.0).astype(BF)
                both.append(jnp.concatenate([head, w[BLK:].astype(BF)], axis=0) if j < events // BLK - 1 else head)
            o = jnp.dot(jnp.concatenate(both, axis=1), v[p, j], preferred_element_type=F32)
            if j == 0:
                att[p, rest, :] = o
            else:
                att[p, rest, :] += o
        return carry

    lax.fori_loop(0, 4, attend, 0)

    def finish(c, carry):
        cols = []
        for i in range(BLK // 128):
            line = slot_ref[pl.ds(c * (BLK // 128) + i, 1), :]
            spread = jnp.where(eye, jnp.broadcast_to(line, (128, 128)), 0)
            cols.append(jnp.sum(spread, axis=1, keepdims=True))
        here = jnp.concatenate(cols, axis=0) >= 0
        at = pl.ds(pl.multiple_of(c * BLK, BLK), BLK)
        full = jnp.concatenate([att[p, at, :] for p in range(4)], axis=1)
        gated = (norm_rows(full, gain_out_ref[...]) * gate[at, :]).astype(BF)
        update = jnp.dot(gated, w_out_ref[...], preferred_element_type=F32) + b_out_ref[...]
        out_ref[at, :] = jnp.where(here, hist[at, :].astype(F32) + update, 0.0).astype(BF)
        done(c, at)
        return carry

    lax.fori_loop(0, events // BLK, finish, 0, unroll=True)


def layer_scratch(events):
    return [
        pltpu.VMEM((events, 512), BF),
        pltpu.VMEM((events, 512), F32),
        pltpu.VMEM((8, events, 128), BF),
        pltpu.VMEM((4, events, 128), BF),
        pltpu.VMEM((4, events // BLK, 2 * BLK, 128), BF),
        pltpu.VMEM((4, events, 128), F32),
    ]


def weight_scratch(weights):
    return [pltpu.VMEM(w.shape, w.dtype) for w in weights] + [pltpu.SemaphoreType.DMA((len(weights),))]


def fetch_kernel(seqs, n_dp, n_table, owners_hbm, rows_hbm, lengths_hbm, dest_hbm, table_hbm, *refs):
    weights_hbm, refs = refs[:6], refs[6:]
    out_hbm = refs[0]
    (owners, rows, lengths, dest, table, local_sem), refs = refs[1:7], refs[7:]
    weights, weight_sem, refs = refs[:6], refs[6], refs[7:]
    (mine, every, req, asked, wanted_rows, wide, picked, parcel, landing, slot_ref, out,
     send_z, recv_z, send_t, recv_t, fetch_sem, send_rows, recv_rows, out_sem), work = refs[:19], refs[19:]
    me_dp, me_t = lax.axis_index("dp"), lax.axis_index("table")
    events = rows.shape[1]
    lines = events // 128

    inputs = [(owners_hbm, owners), (rows_hbm, rows), (lengths_hbm, lengths), (dest_hbm, dest), (table_hbm, table)]
    local = [pltpu.make_async_copy(a, b, local_sem.at[i]) for i, (a, b) in enumerate(inputs)]
    local += [pltpu.make_async_copy(a, b, weight_sem.at[i]) for i, (a, b) in enumerate(zip(weights_hbm, weights))]
    for copy in local:
        copy.start()

    barrier = pltpu.get_barrier_semaphore()
    for i in range(1, n_dp):
        pl.semaphore_signal(barrier, inc=1, device_id={"dp": lax.rem(me_dp + i, n_dp)}, device_id_type=MESH)

    @pl.loop(1, n_table)
    def _(i):
        pl.semaphore_signal(barrier, inc=1, device_id={"table": lax.rem(me_t + i, n_table)}, device_id_type=MESH)

    for copy in local[:4]:
        copy.wait()
    lane = lax.broadcasted_iota(INT, (1, 128), 1)
    for s in range(seqs):
        for r in range(lines):
            cs = slice(r * 128, (r + 1) * 128)
            packed = owners[s, :, cs] * 4096 + rows[s:s + 1, cs]
            mine[s * lines + r:s * lines + r + 1, :] = jnp.where(lane + r * 128 < lengths[s], packed, -1)
    for j in range(8):
        mine[seqs * lines + j:seqs * lines + j + 1, :] = jnp.zeros((1, 128), INT) + dest[0, min(j, seqs - 1)]
    every[me_dp] = mine[...]
    pl.semaphore_wait(barrier, n_dp - 1 + n_table - 1)

    copies = []
    for i in range(1, n_dp):
        copy = pltpu.make_async_remote_copy(
            src_ref=mine, dst_ref=every.at[me_dp], send_sem=send_z.at[i], recv_sem=recv_z.at[me_dp],
            device_id={"dp": lax.rem(me_dp + i, n_dp)}, device_id_type=MESH)
        copy.start()
        copies.append(copy)
    def widen(begin, end):
        @pl.loop(begin, end)
        def _(i):
            at = pl.ds(pl.multiple_of(i * 64, 64), 64)
            wide[at, :] = table[at, :].astype(F32)

    chunks = table.shape[0] // 64
    local[4].wait()
    widen(0, chunks // 2)
    for i in range(1, n_dp):
        pltpu.make_async_remote_copy(
            src_ref=mine, dst_ref=every.at[lax.rem(me_dp + i, n_dp)], send_sem=send_z.at[i],
            recv_sem=recv_z.at[lax.rem(me_dp + i, n_dp)],
            device_id={"dp": lax.rem(me_dp + i, n_dp)}, device_id_type=MESH).wait_recv()

    shard = lax.broadcasted_iota(INT, (n_table, 128), 0)
    place = lax.broadcasted_iota(INT, (128, 128), 0)
    upper = (place <= lax.broadcasted_iota(INT, (128, 128), 1)).astype(F32).astype(BF)
    request = jnp.zeros((2 * n_table, 128), F32)
    for s in range(seqs):
        refs = jnp.zeros((lines, 128), INT)
        for d in range(n_dp):
            for j in range(seqs):
                went = every[d, seqs * lines + j:seqs * lines + j + 1, :]
                refs += jnp.where(went == me_dp * seqs + s, every[d, j * lines:(j + 1) * lines, :], 0)
        owner, row = refs >> 12, refs & 4095
        named = [(jnp.broadcast_to(owner[r:r + 1, :], (n_table, 128)) == shard) for r in range(lines)]
        before = jnp.zeros((n_table, 1), F32)
        for r in range(lines):
            hot = named[r].astype(F32)
            upto = jnp.dot(hot.astype(BF), upper, preferred_element_type=F32) + before
            before += jnp.sum(hot, axis=1, keepdims=True)
            rank = jnp.sum(jnp.where(named[r], upto - 1.0, 0.0), axis=0, keepdims=True)
            slot = jnp.sum(jnp.where(named[r], upto + (shard * SLOTS).astype(F32), 0.0), axis=0, keepdims=True)
            slot_ref[s, r:r + 1, :] = slot.astype(INT) - 1
            high = jnp.broadcast_to(row[r:r + 1, :] >> 6, (n_table, 128)).astype(F32)
            low = jnp.broadcast_to(row[r:r + 1, :] & 63, (n_table, 128)).astype(F32)
            left = jnp.concatenate([jnp.where(named[r], high, 0.0), jnp.where(named[r], low, 0.0)], axis=0)
            right = jnp.broadcast_to(rank.astype(INT) + s * SLOTS, (128, 128)) == place
            request += lax.dot_general(left.astype(BF), right.astype(F32).astype(BF), (((1,), (1,)), ((), ())),
                                       preferred_element_type=F32)
    wanted = (request[:n_table] * 64.0 + request[n_table:]).astype(INT)
    for t in range(n_table):
        req[t] = wanted[t:t + 1, :]
    asked[me_t] = req[me_t]

    @pl.loop(1, n_table)
    def _(i):
        peer = lax.rem(me_t + i, n_table)
        pltpu.make_async_remote_copy(
            src_ref=req.at[peer], dst_ref=asked.at[me_t], send_sem=send_t.at[i], recv_sem=recv_t.at[me_t],
            device_id={"table": peer}, device_id_type=MESH).start()

    widen(chunks // 2, chunks)
    for copy in copies:
        copy.wait_send()

    @pl.loop(1, n_table)
    def _(i):
        peer = lax.rem(me_t + i, n_table)
        pltpu.make_async_remote_copy(
            src_ref=req.at[peer], dst_ref=asked.at[peer], send_sem=send_t.at[i], recv_sem=recv_t.at[peer],
            device_id={"table": peer}, device_id_type=MESH).wait()

    fetch = pltpu.make_async_copy(asked, wanted_rows, fetch_sem)
    fetch.start()
    fetch.wait()

    def part(t):
        return pl.ds(pl.multiple_of(t * SLOTS, SLOTS), SLOTS)

    def pick(s, peer):
        for k in range(SLOTS):
            row = wanted_rows[peer, 0, s * SLOTS + k] & (wide.shape[0] - 1)
            picked[k:k + 1, :] = wide[pl.ds(row, 1), :]

    def row_copy(s, i, peer, other):
        return pltpu.make_async_remote_copy(
            src_ref=parcel.at[s, peer], dst_ref=landing.at[s, part(other)], send_sem=send_rows.at[s, i],
            recv_sem=recv_rows.at[s, other], device_id={"table": peer}, device_id_type=MESH)

    turn = lax.rem(me_t * 7, n_table - 1)
    y0, x0, c0 = me_t // 8, me_t // 2 % 4, me_t % 2

    for s in range(seqs):
        @pl.loop(0, n_table - 1)
        def _(k):
            i = lax.rem(k + turn, n_table - 1) + 1
            peer = (y0 + i // 8) % 4 * 8 + (x0 + i // 2 % 4) % 4 * 2 + (c0 + i % 2) % 2
            pick(s, peer)
            parcel[s, peer] = picked[...].astype(BF)
            row_copy(s, peer, peer, me_t).start()

        pick(s, me_t)
        landing[s, part(me_t), :] = picked[...].astype(BF)

    for copy in local[5:]:
        copy.wait()

    def settle(s):
        @pl.loop(1, n_table)
        def _(i):
            peer = lax.rem(me_t + i, n_table)
            row_copy(s, peer, peer, peer).wait()

    def leave(s, c):
        at = pl.ds(c * BLK, BLK)
        return pltpu.make_async_copy(out.at[s, at], out_hbm.at[s, at], out_sem.at[s, c])

    @pl.loop(0, seqs)
    def _(s):
        settle(s)
        layer_body(slot_ref.at[s], landing.at[s], weights, out.at[s], lambda c, at: leave(s, c).start(), *work)

    for s in range(seqs):
        for c in range(events // BLK):
            leave(s, c).wait()


def fetch_call(n_dp, n_table, owners, rows, lengths, dest, table, weights):
    seqs, events = rows.shape
    lines, width = events // 128, table.shape[1]
    any_space = pl.BlockSpec(memory_space=pl.ANY)
    return pl.pallas_call(
        functools.partial(fetch_kernel, seqs, n_dp, n_table),
        out_shape=jax.ShapeDtypeStruct((seqs, events, width), BF),
        in_specs=[any_space] * (5 + len(weights)),
        out_specs=any_space,
        scratch_shapes=[
            pltpu.VMEM(owners.shape, INT),
            pltpu.VMEM(rows.shape, INT),
            pltpu.SMEM(lengths.shape, INT),
            pltpu.SMEM(dest.shape, INT),
            pltpu.VMEM(table.shape, BF),
            pltpu.SemaphoreType.DMA((5,)),
            *weight_scratch(weights),
            pltpu.VMEM((seqs * lines + 8, 128), INT),
            pltpu.VMEM((n_dp, seqs * lines + 8, 128), INT),
            pltpu.VMEM((n_table, 1, 128), INT),
            pltpu.VMEM((n_table, 1, 128), INT),
            pltpu.SMEM((n_table, 1, 128), INT),
            pltpu.VMEM(table.shape, F32),
            pltpu.VMEM((SLOTS, width), F32),
            pltpu.VMEM((seqs, n_table, SLOTS, width), BF),
            pltpu.VMEM((seqs, n_table * SLOTS, width), BF),
            pltpu.VMEM((seqs, lines, 128), INT),
            pltpu.VMEM((seqs, events, width), BF),
            pltpu.SemaphoreType.DMA((n_dp,)),
            pltpu.SemaphoreType.DMA((n_dp,)),
            pltpu.SemaphoreType.DMA((n_table,)),
            pltpu.SemaphoreType.DMA((n_table,)),
            pltpu.SemaphoreType.DMA,
            pltpu.SemaphoreType.DMA((seqs, n_table)),
            pltpu.SemaphoreType.DMA((seqs, n_table)),
            pltpu.SemaphoreType.DMA((seqs, events // BLK)),
            *layer_scratch(events),
        ],
        compiler_params=pltpu.CompilerParams(collective_id=0, has_side_effects=True, vmem_limit_bytes=60 << 20),
        name="fetch",
    )(owners, rows, lengths, dest, table, *weights)


def on_device(owners, local_rows, lengths, destinations, table, gain_in, w_in, b_in, gain_out, w_out, b_out):
    seqs, events = local_rows.shape
    n_dp, n_table = lax.axis_size("dp"), lax.axis_size("table")
    weights = (gain_in[None], w_in, b_in[None], gain_out[None], w_out, b_out[None])
    return fetch_call(
        n_dp, n_table, owners.reshape(seqs, 1, events), local_rows, lengths, destinations, table, weights)


def solution(mesh):
    placed = (
        P(("dp", "table"), None, None),
        P(("dp", "table"), None),
        P(("dp", "table")),
        P("table", "dp"),
        P("table", None),
        P(),
        P(),
        P(),
        P(),
        P(),
        P(),
    )
    return jax.shard_map(
        on_device,
        mesh=mesh,
        in_specs=placed,
        out_specs=P(("dp", "table"), None, None),
        check_vma=False,
    )
```

```python
import functools
import jax
import jax.numpy as jnp
from jax import lax
from jax.experimental import pallas as pl
from jax.experimental.pallas import tpu as pltpu
from jax.sharding import PartitionSpec as P

HEADS = 8
EPS = 1e-05
BLK = 256
BF = jnp.bfloat16
F32 = jnp.float32
INT = jnp.int32
MESH = pl.DeviceIdType.MESH
SLOTS = 48


def silu_half(u):
    return u + u * jnp.tanh(u)


def norm_rows(values, gain):
    centre = jnp.mean(values, axis=-1, keepdims=True)
    spread = values - centre
    variance = jnp.mean(spread * spread, axis=-1, keepdims=True)
    return spread * lax.rsqrt(variance + EPS) * gain


def layer_body(slot_ref, rows_ref, weights, out_ref, done, hist, gate, q, k, v, att):
    gain_in_ref, w_in_ref, b_in_ref, gain_out_ref, w_out_ref, b_out_ref = weights
    events, width = hist.shape
    slots = rows_ref.shape[0]
    lanes = lax.broadcasted_iota(jnp.int32, (128, 128), 1)
    subs = lax.broadcasted_iota(jnp.int32, (128, 128), 0)
    eye = lanes == subs
    half = lax.broadcasted_iota(jnp.int32, (BLK, 128), 1) < 64

    def project(c, carry):
        cols = []
        for i in range(BLK // 128):
            line = slot_ref[pl.ds(c * (BLK // 128) + i, 1), :]
            spread = jnp.where(eye, jnp.broadcast_to(line, (128, 128)), 0)
            cols.append(jnp.sum(spread, axis=1, keepdims=True))
        col = jnp.concatenate(cols, axis=0)
        here = (col >= 0).astype(F32)
        pick = (col == lax.broadcasted_iota(jnp.int32, (BLK, slots), 1)).astype(F32).astype(BF)
        rows = jnp.dot(pick, rows_ref[...], preferred_element_type=F32)
        at = pl.ds(pl.multiple_of(c * BLK, BLK), BLK)
        hist[at, :] = rows.astype(BF)
        normed = norm_rows(rows, gain_in_ref[...] * 0.5).astype(BF)
        for part in range(4):
            cs = slice(part * width, (part + 1) * width)
            pre = jnp.dot(normed, w_in_ref[:, cs], preferred_element_type=F32) + b_in_ref[:, cs] * 0.5
            act = silu_half(pre)
            if part == 0:
                gate[at, :] = act
            elif part == 1:
                act = act * here
                for p in range(4):
                    piece = act[:, p * 128:(p + 1) * 128]
                    v[p, c, :BLK, :] = jnp.where(half, piece, 0.0).astype(BF)
                    v[p, c, BLK:, :] = jnp.where(half, 0.0, piece).astype(BF)
            else:
                for p in range(4):
                    piece = act[:, p * 128:(p + 1) * 128]
                    if part == 3:
                        k[p, at, :] = piece.astype(BF)
                    else:
                        piece = piece * 0.0625
                        q[2 * p, at, :] = jnp.where(half, piece, 0.0).astype(BF)
                        q[2 * p + 1, at, :] = jnp.where(half, 0.0, piece).astype(BF)
        return carry

    lax.fori_loop(0, events // BLK, project, 0, unroll=True)

    tri = lax.broadcasted_iota(jnp.int32, (BLK, BLK), 0) >= lax.broadcasted_iota(jnp.int32, (BLK, BLK), 1)

    def attend(p, carry):
        for j in range(events // BLK):
            ks = slice(j * BLK, (j + 1) * BLK)
            rest = slice(j * BLK, events)
            both = []
            for h in range(2):
                s = lax.dot_general(q[2 * p + h, rest, :], k[p, ks, :], (((1,), (1,)), ((), ())), preferred_element_type=F32)
                w = silu_half(s)
                head = jnp.where(tri, w[:BLK], 0.0).astype(BF)
                both.append(jnp.concatenate([head, w[BLK:].astype(BF)], axis=0) if j < events // BLK - 1 else head)
            o = jnp.dot(jnp.concatenate(both, axis=1), v[p, j], preferred_element_type=F32)
            if j == 0:
                att[p, rest, :] = o
            else:
                att[p, rest, :] += o
        return carry

    lax.fori_loop(0, 4, attend, 0)

    def finish(c, carry):
        cols = []
        for i in range(BLK // 128):
            line = slot_ref[pl.ds(c * (BLK // 128) + i, 1), :]
            spread = jnp.where(eye, jnp.broadcast_to(line, (128, 128)), 0)
            cols.append(jnp.sum(spread, axis=1, keepdims=True))
        here = jnp.concatenate(cols, axis=0) >= 0
        at = pl.ds(pl.multiple_of(c * BLK, BLK), BLK)
        full = jnp.concatenate([att[p, at, :] for p in range(4)], axis=1)
        gated = (norm_rows(full, gain_out_ref[...]) * gate[at, :]).astype(BF)
        update = jnp.dot(gated, w_out_ref[...], preferred_element_type=F32) + b_out_ref[...]
        out_ref[at, :] = jnp.where(here, hist[at, :].astype(F32) + update, 0.0).astype(BF)
        done(c, at)
        return carry

    lax.fori_loop(0, events // BLK, finish, 0, unroll=True)


def layer_scratch(events):
    return [
        pltpu.VMEM((events, 512), BF),
        pltpu.VMEM((events, 512), F32),
        pltpu.VMEM((8, events, 128), BF),
        pltpu.VMEM((4, events, 128), BF),
        pltpu.VMEM((4, events // BLK, 2 * BLK, 128), BF),
        pltpu.VMEM((4, events, 128), F32),
    ]


def weight_scratch(weights):
    return [pltpu.VMEM(w.shape, w.dtype) for w in weights] + [pltpu.SemaphoreType.DMA((len(weights),))]


def fetch_kernel(seqs, n_dp, n_table, owners_hbm, rows_hbm, lengths_hbm, dest_hbm, table_hbm, *refs):
    weights_hbm, refs = refs[:6], refs[6:]
    out_hbm = refs[0]
    (owners, rows, lengths, dest, table, local_sem), refs = refs[1:7], refs[7:]
    weights, weight_sem, refs = refs[:6], refs[6], refs[7:]
    (mine, every, req, asked, wanted_rows, wide, picked, parcel, landing, slot_ref, out,
     send_z, recv_z, send_t, recv_t, fetch_sem, send_rows, recv_rows, out_sem), work = refs[:19], refs[19:]
    me_dp, me_t = lax.axis_index("dp"), lax.axis_index("table")
    events = rows.shape[1]
    lines = events // 128

    inputs = [(owners_hbm, owners), (rows_hbm, rows), (lengths_hbm, lengths), (dest_hbm, dest), (table_hbm, table)]
    local = [pltpu.make_async_copy(a, b, local_sem.at[i]) for i, (a, b) in enumerate(inputs)]
    local += [pltpu.make_async_copy(a, b, weight_sem.at[i]) for i, (a, b) in enumerate(zip(weights_hbm, weights))]
    for copy in local:
        copy.start()

    barrier = pltpu.get_barrier_semaphore()
    for i in range(1, n_dp):
        pl.semaphore_signal(barrier, inc=1, device_id={"dp": lax.rem(me_dp + i, n_dp)}, device_id_type=MESH)

    @pl.loop(1, n_table)
    def _(i):
        pl.semaphore_signal(barrier, inc=1, device_id={"table": lax.rem(me_t + i, n_table)}, device_id_type=MESH)

    for copy in local[:4]:
        copy.wait()
    lane = lax.broadcasted_iota(INT, (1, 128), 1)
    for s in range(seqs):
        for r in range(lines):
            cs = slice(r * 128, (r + 1) * 128)
            packed = owners[s, :, cs] * 4096 + rows[s:s + 1, cs]
            mine[s * lines + r:s * lines + r + 1, :] = jnp.where(lane + r * 128 < lengths[s], packed, -1)
    for j in range(8):
        mine[seqs * lines + j:seqs * lines + j + 1, :] = jnp.zeros((1, 128), INT) + dest[0, min(j, seqs - 1)]
    every[me_dp] = mine[...]
    pl.semaphore_wait(barrier, n_dp - 1 + n_table - 1)

    copies = []
    for i in range(1, n_dp):
        copy = pltpu.make_async_remote_copy(
            src_ref=mine, dst_ref=every.at[me_dp], send_sem=send_z.at[i], recv_sem=recv_z.at[me_dp],
            device_id={"dp": lax.rem(me_dp + i, n_dp)}, device_id_type=MESH)
        copy.start()
        copies.append(copy)
    def widen(begin, end):
        @pl.loop(begin, end)
        def _(i):
            at = pl.ds(pl.multiple_of(i * 64, 64), 64)
            wide[at, :] = table[at, :].astype(F32)

    chunks = table.shape[0] // 64
    local[4].wait()
    widen(0, chunks // 2)
    for i in range(1, n_dp):
        pltpu.make_async_remote_copy(
            src_ref=mine, dst_ref=every.at[lax.rem(me_dp + i, n_dp)], send_sem=send_z.at[i],
            recv_sem=recv_z.at[lax.rem(me_dp + i, n_dp)],
            device_id={"dp": lax.rem(me_dp + i, n_dp)}, device_id_type=MESH).wait_recv()

    shard = lax.broadcasted_iota(INT, (n_table, 128), 0)
    place = lax.broadcasted_iota(INT, (128, 128), 0)
    upper = (place <= lax.broadcasted_iota(INT, (128, 128), 1)).astype(F32).astype(BF)
    request = jnp.zeros((2 * n_table, 128), F32)
    for s in range(seqs):
        refs = jnp.zeros((lines, 128), INT)
        for d in range(n_dp):
            for j in range(seqs):
                went = every[d, seqs * lines + j:seqs * lines + j + 1, :]
                refs += jnp.where(went == me_dp * seqs + s, every[d, j * lines:(j + 1) * lines, :], 0)
        owner, row = refs >> 12, refs & 4095
        named = [(jnp.broadcast_to(owner[r:r + 1, :], (n_table, 128)) == shard) for r in range(lines)]
        before = jnp.zeros((n_table, 1), F32)
        for r in range(lines):
            hot = named[r].astype(F32)
            upto = jnp.dot(hot.astype(BF), upper, preferred_element_type=F32) + before
            before += jnp.sum(hot, axis=1, keepdims=True)
            rank = jnp.sum(jnp.where(named[r], upto - 1.0, 0.0), axis=0, keepdims=True)
            slot = jnp.sum(jnp.where(named[r], upto + (shard * SLOTS).astype(F32), 0.0), axis=0, keepdims=True)
            slot_ref[s, r:r + 1, :] = slot.astype(INT) - 1
            high = jnp.broadcast_to(row[r:r + 1, :] >> 6, (n_table, 128)).astype(F32)
            low = jnp.broadcast_to(row[r:r + 1, :] & 63, (n_table, 128)).astype(F32)
            left = jnp.concatenate([jnp.where(named[r], high, 0.0), jnp.where(named[r], low, 0.0)], axis=0)
            right = jnp.broadcast_to(rank.astype(INT) + s * SLOTS, (128, 128)) == place
            request += lax.dot_general(left.astype(BF), right.astype(F32).astype(BF), (((1,), (1,)), ((), ())),
                                       preferred_element_type=F32)
    wanted = (request[:n_table] * 64.0 + request[n_table:]).astype(INT)
    for t in range(n_table):
        req[t] = wanted[t:t + 1, :]
    asked[me_t] = req[me_t]

    @pl.loop(1, n_table)
    def _(i):
        peer = lax.rem(me_t + i, n_table)
        pltpu.make_async_remote_copy(
            src_ref=req.at[peer], dst_ref=asked.at[me_t], send_sem=send_t.at[i], recv_sem=recv_t.at[me_t],
            device_id={"table": peer}, device_id_type=MESH).start()

    widen(chunks // 2, chunks)
    for copy in copies:
        copy.wait_send()

    @pl.loop(1, n_table)
    def _(i):
        peer = lax.rem(me_t + i, n_table)
        pltpu.make_async_remote_copy(
            src_ref=req.at[peer], dst_ref=asked.at[peer], send_sem=send_t.at[i], recv_sem=recv_t.at[peer],
            device_id={"table": peer}, device_id_type=MESH).wait()

    fetch = pltpu.make_async_copy(asked, wanted_rows, fetch_sem)
    fetch.start()
    fetch.wait()

    def part(t):
        return pl.ds(pl.multiple_of(t * SLOTS, SLOTS), SLOTS)

    def pick(s, peer):
        for k in range(SLOTS):
            row = wanted_rows[peer, 0, s * SLOTS + k] & (wide.shape[0] - 1)
            picked[k:k + 1, :] = wide[pl.ds(row, 1), :]

    def row_copy(s, i, peer, other):
        return pltpu.make_async_remote_copy(
            src_ref=parcel.at[s, peer], dst_ref=landing.at[s, part(other)], send_sem=send_rows.at[s, i],
            recv_sem=recv_rows.at[s, other], device_id={"table": peer}, device_id_type=MESH)

    turn = lax.rem(me_t * 11, n_table - 1)
    y0, x0, c0 = me_t // 8, me_t // 2 % 4, me_t % 2

    for s in range(seqs):
        @pl.loop(0, n_table - 1)
        def _(k):
            i = lax.rem(k * 3 + turn, n_table - 1) + 1
            peer = (y0 + i // 8) % 4 * 8 + (x0 + i // 2 % 4) % 4 * 2 + (c0 + i % 2) % 2
            pick(s, peer)
            parcel[s, peer] = picked[...].astype(BF)
            row_copy(s, peer, peer, me_t).start()

        pick(s, me_t)
        landing[s, part(me_t), :] = picked[...].astype(BF)

    for copy in local[5:]:
        copy.wait()

    def settle(s):
        @pl.loop(1, n_table)
        def _(i):
            peer = lax.rem(me_t + i, n_table)
            row_copy(s, peer, peer, peer).wait()

    def leave(s, c):
        at = pl.ds(c * BLK, BLK)
        return pltpu.make_async_copy(out.at[s, at], out_hbm.at[s, at], out_sem.at[s, c])

    @pl.loop(0, seqs)
    def _(s):
        settle(s)
        layer_body(slot_ref.at[s], landing.at[s], weights, out.at[s], lambda c, at: leave(s, c).start(), *work)

    for s in range(seqs):
        for c in range(events // BLK):
            leave(s, c).wait()


def fetch_call(n_dp, n_table, owners, rows, lengths, dest, table, weights):
    seqs, events = rows.shape
    lines, width = events // 128, table.shape[1]
    any_space = pl.BlockSpec(memory_space=pl.ANY)
    return pl.pallas_call(
        functools.partial(fetch_kernel, seqs, n_dp, n_table),
        out_shape=jax.ShapeDtypeStruct((seqs, events, width), BF),
        in_specs=[any_space] * (5 + len(weights)),
        out_specs=any_space,
        scratch_shapes=[
            pltpu.VMEM(owners.shape, INT),
            pltpu.VMEM(rows.shape, INT),
            pltpu.SMEM(lengths.shape, INT),
            pltpu.SMEM(dest.shape, INT),
            pltpu.VMEM(table.shape, BF),
            pltpu.SemaphoreType.DMA((5,)),
            *weight_scratch(weights),
            pltpu.VMEM((seqs * lines + 8, 128), INT),
            pltpu.VMEM((n_dp, seqs * lines + 8, 128), INT),
            pltpu.VMEM((n_table, 1, 128), INT),
            pltpu.VMEM((n_table, 1, 128), INT),
            pltpu.SMEM((n_table, 1, 128), INT),
            pltpu.VMEM(table.shape, F32),
            pltpu.VMEM((SLOTS, width), F32),
            pltpu.VMEM((seqs, n_table, SLOTS, width), BF),
            pltpu.VMEM((seqs, n_table * SLOTS, width), BF),
            pltpu.VMEM((seqs, lines, 128), INT),
            pltpu.VMEM((seqs, events, width), BF),
            pltpu.SemaphoreType.DMA((n_dp,)),
            pltpu.SemaphoreType.DMA((n_dp,)),
            pltpu.SemaphoreType.DMA((n_table,)),
            pltpu.SemaphoreType.DMA((n_table,)),
            pltpu.SemaphoreType.DMA,
            pltpu.SemaphoreType.DMA((seqs, n_table)),
            pltpu.SemaphoreType.DMA((seqs, n_table)),
            pltpu.SemaphoreType.DMA((seqs, events // BLK)),
            *layer_scratch(events),
        ],
        compiler_params=pltpu.CompilerParams(collective_id=0, has_side_effects=True, vmem_limit_bytes=60 << 20),
        name="fetch",
    )(owners, rows, lengths, dest, table, *weights)


def on_device(owners, local_rows, lengths, destinations, table, gain_in, w_in, b_in, gain_out, w_out, b_out):
    seqs, events = local_rows.shape
    n_dp, n_table = lax.axis_size("dp"), lax.axis_size("table")
    weights = (gain_in[None], w_in, b_in[None], gain_out[None], w_out, b_out[None])
    return fetch_call(
        n_dp, n_table, owners.reshape(seqs, 1, events), local_rows, lengths, destinations, table, weights)


def solution(mesh):
    placed = (
        P(("dp", "table"), None, None),
        P(("dp", "table"), None),
        P(("dp", "table")),
        P("table", "dp"),
        P("table", None),
        P(),
        P(),
        P(),
        P(),
        P(),
        P(),
    )
    return jax.shard_map(
        on_device,
        mesh=mesh,
        in_specs=placed,
        out_specs=P(("dp", "table"), None, None),
        check_vma=False,
    )
```

```python
import functools
import jax
import jax.numpy as jnp
from jax import lax
from jax.experimental import pallas as pl
from jax.experimental.pallas import tpu as pltpu
from jax.sharding import PartitionSpec as P

HEADS = 8
EPS = 1e-05
BLK = 256
BF = jnp.bfloat16
F32 = jnp.float32
INT = jnp.int32
MESH = pl.DeviceIdType.MESH
SLOTS = 48


def silu_half(u):
    return u + u * jnp.tanh(u)


def norm_rows(values, gain):
    centre = jnp.mean(values, axis=-1, keepdims=True)
    spread = values - centre
    variance = jnp.mean(spread * spread, axis=-1, keepdims=True)
    return spread * lax.rsqrt(variance + EPS) * gain


def layer_body(slot_ref, rows_ref, weights, out_ref, done, hist, gate, q, k, v, att):
    gain_in_ref, w_in_ref, b_in_ref, gain_out_ref, w_out_ref, b_out_ref = weights
    events, width = hist.shape
    slots = rows_ref.shape[0]
    lanes = lax.broadcasted_iota(jnp.int32, (128, 128), 1)
    subs = lax.broadcasted_iota(jnp.int32, (128, 128), 0)
    eye = lanes == subs
    half = lax.broadcasted_iota(jnp.int32, (BLK, 128), 1) < 64

    def project(c, carry):
        cols = []
        for i in range(BLK // 128):
            line = slot_ref[pl.ds(c * (BLK // 128) + i, 1), :]
            spread = jnp.where(eye, jnp.broadcast_to(line, (128, 128)), 0)
            cols.append(jnp.sum(spread, axis=1, keepdims=True))
        col = jnp.concatenate(cols, axis=0)
        here = (col >= 0).astype(F32)
        pick = (col == lax.broadcasted_iota(jnp.int32, (BLK, slots), 1)).astype(F32).astype(BF)
        rows = jnp.dot(pick, rows_ref[...], preferred_element_type=F32)
        at = pl.ds(pl.multiple_of(c * BLK, BLK), BLK)
        hist[at, :] = rows.astype(BF)
        normed = norm_rows(rows, gain_in_ref[...] * 0.5).astype(BF)
        for part in range(4):
            cs = slice(part * width, (part + 1) * width)
            pre = jnp.dot(normed, w_in_ref[:, cs], preferred_element_type=F32) + b_in_ref[:, cs] * 0.5
            act = silu_half(pre)
            if part == 0:
                gate[at, :] = act
            elif part == 1:
                act = act * here
                for p in range(4):
                    piece = act[:, p * 128:(p + 1) * 128]
                    v[p, c, :BLK, :] = jnp.where(half, piece, 0.0).astype(BF)
                    v[p, c, BLK:, :] = jnp.where(half, 0.0, piece).astype(BF)
            else:
                for p in range(4):
                    piece = act[:, p * 128:(p + 1) * 128]
                    if part == 3:
                        k[p, at, :] = piece.astype(BF)
                    else:
                        piece = piece * 0.0625
                        q[2 * p, at, :] = jnp.where(half, piece, 0.0).astype(BF)
                        q[2 * p + 1, at, :] = jnp.where(half, 0.0, piece).astype(BF)
        return carry

    lax.fori_loop(0, events // BLK, project, 0, unroll=True)

    tri = lax.broadcasted_iota(jnp.int32, (BLK, BLK), 0) >= lax.broadcasted_iota(jnp.int32, (BLK, BLK), 1)

    def attend(p, carry):
        for j in range(events // BLK):
            ks = slice(j * BLK, (j + 1) * BLK)
            rest = slice(j * BLK, events)
            both = []
            for h in range(2):
                s = lax.dot_general(q[2 * p + h, rest, :], k[p, ks, :], (((1,), (1,)), ((), ())), preferred_element_type=F32)
                w = silu_half(s)
                head = jnp.where(tri, w[:BLK], 0.0).astype(BF)
                both.append(jnp.concatenate([head, w[BLK:].astype(BF)], axis=0) if j < events // BLK - 1 else head)
            o = jnp.dot(jnp.concatenate(both, axis=1), v[p, j], preferred_element_type=F32)
            if j == 0:
                att[p, rest, :] = o
            else:
                att[p, rest, :] += o
        return carry

    lax.fori_loop(0, 4, attend, 0)

    def finish(c, carry):
        cols = []
        for i in range(BLK // 128):
            line = slot_ref[pl.ds(c * (BLK // 128) + i, 1), :]
            spread = jnp.where(eye, jnp.broadcast_to(line, (128, 128)), 0)
            cols.append(jnp.sum(spread, axis=1, keepdims=True))
        here = jnp.concatenate(cols, axis=0) >= 0
        at = pl.ds(pl.multiple_of(c * BLK, BLK), BLK)
        full = jnp.concatenate([att[p, at, :] for p in range(4)], axis=1)
        gated = (norm_rows(full, gain_out_ref[...]) * gate[at, :]).astype(BF)
        update = jnp.dot(gated, w_out_ref[...], preferred_element_type=F32) + b_out_ref[...]
        out_ref[at, :] = jnp.where(here, hist[at, :].astype(F32) + update, 0.0).astype(BF)
        done(c, at)
        return carry

    lax.fori_loop(0, events // BLK, finish, 0, unroll=True)


def layer_scratch(events):
    return [
        pltpu.VMEM((events, 512), BF),
        pltpu.VMEM((events, 512), F32),
        pltpu.VMEM((8, events, 128), BF),
        pltpu.VMEM((4, events, 128), BF),
        pltpu.VMEM((4, events // BLK, 2 * BLK, 128), BF),
        pltpu.VMEM((4, events, 128), F32),
    ]


def weight_scratch(weights):
    return [pltpu.VMEM(w.shape, w.dtype) for w in weights] + [pltpu.SemaphoreType.DMA((len(weights),))]


def fetch_kernel(seqs, n_dp, n_table, owners_hbm, rows_hbm, lengths_hbm, dest_hbm, table_hbm, *refs):
    weights_hbm, refs = refs[:6], refs[6:]
    out_hbm = refs[0]
    (owners, rows, lengths, dest, table, local_sem), refs = refs[1:7], refs[7:]
    weights, weight_sem, refs = refs[:6], refs[6], refs[7:]
    (mine, every, req, asked, wanted_rows, wide, picked, parcel, landing, slot_ref, out,
     send_z, recv_z, send_t, recv_t, fetch_sem, send_rows, recv_rows, out_sem), work = refs[:19], refs[19:]
    me_dp, me_t = lax.axis_index("dp"), lax.axis_index("table")
    events = rows.shape[1]
    lines = events // 128

    inputs = [(owners_hbm, owners), (rows_hbm, rows), (lengths_hbm, lengths), (dest_hbm, dest), (table_hbm, table)]
    local = [pltpu.make_async_copy(a, b, local_sem.at[i]) for i, (a, b) in enumerate(inputs)]
    local += [pltpu.make_async_copy(a, b, weight_sem.at[i]) for i, (a, b) in enumerate(zip(weights_hbm, weights))]
    for copy in local:
        copy.start()

    barrier = pltpu.get_barrier_semaphore()
    for i in range(1, n_dp):
        pl.semaphore_signal(barrier, inc=1, device_id={"dp": lax.rem(me_dp + i, n_dp)}, device_id_type=MESH)

    @pl.loop(1, n_table)
    def _(i):
        pl.semaphore_signal(barrier, inc=1, device_id={"table": lax.rem(me_t + i, n_table)}, device_id_type=MESH)

    for copy in local[:4]:
        copy.wait()
    lane = lax.broadcasted_iota(INT, (1, 128), 1)
    for s in range(seqs):
        for r in range(lines):
            cs = slice(r * 128, (r + 1) * 128)
            packed = owners[s, :, cs] * 4096 + rows[s:s + 1, cs]
            mine[s * lines + r:s * lines + r + 1, :] = jnp.where(lane + r * 128 < lengths[s], packed, -1)
    for j in range(8):
        mine[seqs * lines + j:seqs * lines + j + 1, :] = jnp.zeros((1, 128), INT) + dest[0, min(j, seqs - 1)]
    every[me_dp] = mine[...]
    pl.semaphore_wait(barrier, n_dp - 1 + n_table - 1)

    copies = []
    for i in range(1, n_dp):
        copy = pltpu.make_async_remote_copy(
            src_ref=mine, dst_ref=every.at[me_dp], send_sem=send_z.at[i], recv_sem=recv_z.at[me_dp],
            device_id={"dp": lax.rem(me_dp + i, n_dp)}, device_id_type=MESH)
        copy.start()
        copies.append(copy)
    def widen(begin, end):
        @pl.loop(begin, end)
        def _(i):
            at = pl.ds(pl.multiple_of(i * 64, 64), 64)
            wide[at, :] = table[at, :].astype(F32)

    chunks = table.shape[0] // 64
    local[4].wait()
    widen(0, chunks // 2)
    for i in range(1, n_dp):
        pltpu.make_async_remote_copy(
            src_ref=mine, dst_ref=every.at[lax.rem(me_dp + i, n_dp)], send_sem=send_z.at[i],
            recv_sem=recv_z.at[lax.rem(me_dp + i, n_dp)],
            device_id={"dp": lax.rem(me_dp + i, n_dp)}, device_id_type=MESH).wait_recv()

    shard = lax.broadcasted_iota(INT, (n_table, 128), 0)
    place = lax.broadcasted_iota(INT, (128, 128), 0)
    upper = (place <= lax.broadcasted_iota(INT, (128, 128), 1)).astype(F32).astype(BF)
    request = jnp.zeros((2 * n_table, 128), F32)
    for s in range(seqs):
        refs = jnp.zeros((lines, 128), INT)
        for d in range(n_dp):
            for j in range(seqs):
                went = every[d, seqs * lines + j:seqs * lines + j + 1, :]
                refs += jnp.where(went == me_dp * seqs + s, every[d, j * lines:(j + 1) * lines, :], 0)
        owner, row = refs >> 12, refs & 4095
        named = [(jnp.broadcast_to(owner[r:r + 1, :], (n_table, 128)) == shard) for r in range(lines)]
        before = jnp.zeros((n_table, 1), F32)
        for r in range(lines):
            hot = named[r].astype(F32)
            upto = jnp.dot(hot.astype(BF), upper, preferred_element_type=F32) + before
            before += jnp.sum(hot, axis=1, keepdims=True)
            rank = jnp.sum(jnp.where(named[r], upto - 1.0, 0.0), axis=0, keepdims=True)
            slot = jnp.sum(jnp.where(named[r], upto + (shard * SLOTS).astype(F32), 0.0), axis=0, keepdims=True)
            slot_ref[s, r:r + 1, :] = slot.astype(INT) - 1
            high = jnp.broadcast_to(row[r:r + 1, :] >> 6, (n_table, 128)).astype(F32)
            low = jnp.broadcast_to(row[r:r + 1, :] & 63, (n_table, 128)).astype(F32)
            left = jnp.concatenate([jnp.where(named[r], high, 0.0), jnp.where(named[r], low, 0.0)], axis=0)
            right = jnp.broadcast_to(rank.astype(INT) + s * SLOTS, (128, 128)) == place
            request += lax.dot_general(left.astype(BF), right.astype(F32).astype(BF), (((1,), (1,)), ((), ())),
                                       preferred_element_type=F32)
    wanted = (request[:n_table] * 64.0 + request[n_table:]).astype(INT)
    for t in range(n_table):
        req[t] = wanted[t:t + 1, :]
    asked[me_t] = req[me_t]

    @pl.loop(1, n_table)
    def _(i):
        peer = lax.rem(me_t + i, n_table)
        pltpu.make_async_remote_copy(
            src_ref=req.at[peer], dst_ref=asked.at[me_t], send_sem=send_t.at[i], recv_sem=recv_t.at[me_t],
            device_id={"table": peer}, device_id_type=MESH).start()

    widen(chunks // 2, chunks)
    for copy in copies:
        copy.wait_send()

    @pl.loop(1, n_table)
    def _(i):
        peer = lax.rem(me_t + i, n_table)
        pltpu.make_async_remote_copy(
            src_ref=req.at[peer], dst_ref=asked.at[peer], send_sem=send_t.at[i], recv_sem=recv_t.at[peer],
            device_id={"table": peer}, device_id_type=MESH).wait()

    fetch = pltpu.make_async_copy(asked, wanted_rows, fetch_sem)
    fetch.start()
    fetch.wait()

    def part(t):
        return pl.ds(pl.multiple_of(t * SLOTS, SLOTS), SLOTS)

    def pick(s, peer):
        for k in range(SLOTS):
            row = wanted_rows[peer, 0, s * SLOTS + k] & (wide.shape[0] - 1)
            picked[k:k + 1, :] = wide[pl.ds(row, 1), :]

    def row_copy(s, i, peer, other):
        return pltpu.make_async_remote_copy(
            src_ref=parcel.at[s, peer], dst_ref=landing.at[s, part(other)], send_sem=send_rows.at[s, i],
            recv_sem=recv_rows.at[s, other], device_id={"table": peer}, device_id_type=MESH)

    turn = lax.rem(me_t * 11, n_table - 1)
    y0, x0, c0 = me_t // 8, me_t // 2 % 4, me_t % 2

    for s in range(seqs):
        @pl.loop(0, n_table - 1)
        def _(k):
            i = lax.rem(k * 5 + turn, n_table - 1) + 1
            peer = (y0 + i // 8) % 4 * 8 + (x0 + i // 2 % 4) % 4 * 2 + (c0 + i % 2) % 2
            pick(s, peer)
            parcel[s, peer] = picked[...].astype(BF)
            row_copy(s, peer, peer, me_t).start()

        pick(s, me_t)
        landing[s, part(me_t), :] = picked[...].astype(BF)

    for copy in local[5:]:
        copy.wait()

    def settle(s):
        @pl.loop(1, n_table)
        def _(i):
            peer = lax.rem(me_t + i, n_table)
            row_copy(s, peer, peer, peer).wait()

    def leave(s, c):
        at = pl.ds(c * BLK, BLK)
        return pltpu.make_async_copy(out.at[s, at], out_hbm.at[s, at], out_sem.at[s, c])

    @pl.loop(0, seqs)
    def _(s):
        settle(s)
        layer_body(slot_ref.at[s], landing.at[s], weights, out.at[s], lambda c, at: leave(s, c).start(), *work)

    for s in range(seqs):
        for c in range(events // BLK):
            leave(s, c).wait()


def fetch_call(n_dp, n_table, owners, rows, lengths, dest, table, weights):
    seqs, events = rows.shape
    lines, width = events // 128, table.shape[1]
    any_space = pl.BlockSpec(memory_space=pl.ANY)
    return pl.pallas_call(
        functools.partial(fetch_kernel, seqs, n_dp, n_table),
        out_shape=jax.ShapeDtypeStruct((seqs, events, width), BF),
        in_specs=[any_space] * (5 + len(weights)),
        out_specs=any_space,
        scratch_shapes=[
            pltpu.VMEM(owners.shape, INT),
            pltpu.VMEM(rows.shape, INT),
            pltpu.SMEM(lengths.shape, INT),
            pltpu.SMEM(dest.shape, INT),
            pltpu.VMEM(table.shape, BF),
            pltpu.SemaphoreType.DMA((5,)),
            *weight_scratch(weights),
            pltpu.VMEM((seqs * lines + 8, 128), INT),
            pltpu.VMEM((n_dp, seqs * lines + 8, 128), INT),
            pltpu.VMEM((n_table, 1, 128), INT),
            pltpu.VMEM((n_table, 1, 128), INT),
            pltpu.SMEM((n_table, 1, 128), INT),
            pltpu.VMEM(table.shape, F32),
            pltpu.VMEM((SLOTS, width), F32),
            pltpu.VMEM((seqs, n_table, SLOTS, width), BF),
            pltpu.VMEM((seqs, n_table * SLOTS, width), BF),
            pltpu.VMEM((seqs, lines, 128), INT),
            pltpu.VMEM((seqs, events, width), BF),
            pltpu.SemaphoreType.DMA((n_dp,)),
            pltpu.SemaphoreType.DMA((n_dp,)),
            pltpu.SemaphoreType.DMA((n_table,)),
            pltpu.SemaphoreType.DMA((n_table,)),
            pltpu.SemaphoreType.DMA,
            pltpu.SemaphoreType.DMA((seqs, n_table)),
            pltpu.SemaphoreType.DMA((seqs, n_table)),
            pltpu.SemaphoreType.DMA((seqs, events // BLK)),
            *layer_scratch(events),
        ],
        compiler_params=pltpu.CompilerParams(collective_id=0, has_side_effects=True, vmem_limit_bytes=60 << 20),
        name="fetch",
    )(owners, rows, lengths, dest, table, *weights)


def on_device(owners, local_rows, lengths, destinations, table, gain_in, w_in, b_in, gain_out, w_out, b_out):
    seqs, events = local_rows.shape
    n_dp, n_table = lax.axis_size("dp"), lax.axis_size("table")
    weights = (gain_in[None], w_in, b_in[None], gain_out[None], w_out, b_out[None])
    return fetch_call(
        n_dp, n_table, owners.reshape(seqs, 1, events), local_rows, lengths, destinations, table, weights)


def solution(mesh):
    placed = (
        P(("dp", "table"), None, None),
        P(("dp", "table"), None),
        P(("dp", "table")),
        P("table", "dp"),
        P("table", None),
        P(),
        P(),
        P(),
        P(),
        P(),
        P(),
    )
    return jax.shard_map(
        on_device,
        mesh=mesh,
        in_specs=placed,
        out_specs=P(("dp", "table"), None, None),
        check_vma=False,
    )
```
